512 devices in a mesh: row: 8 (over y, core), col: 8 (over x, z_hi), depth: 8 (over z_lo).
Axes of the slice: x: 4, y: 4, z: 16 (z_hi: 2, z_lo: 8; z = z_hi * 8 + z_lo), core: 2. Of those that a mesh axis runs over, the one named last changes fastest.
Arguments:
- layer_input: bfloat16 [4096, 5120], P('depth', 'row'), may hold values from -6 to 6
- output_grad: bfloat16 [4096, 5120], P('depth', 'row'), may hold values from -6 to 6
- w_gate: bfloat16 [5120, 7168], P('row', 'col'), may hold values from -0.078125 to 0.078125
- w_up: bfloat16 [5120, 7168], P('row', 'col'), may hold values from -0.078125 to 0.078125
- w_down: bfloat16 [7168, 5120], P('col', 'row'), may hold values from -0.0625 to 0.0625
Outputs:
- input_grad: float32 [4096, 5120], P('depth', 'row')
- gate_grad: float32 [5120, 7168], P(('row', 'depth'), 'col')
- up_grad: float32 [5120, 7168], P(('row', 'depth'), 'col')
- down_grad: float32 [7168, 5120], P('col', ('row', 'depth'))
The draws below stay inside these ranges and needn't reach their ends.
All inputs are finite; a program needn't handle non-finite values.
Results may differ from the reference program's by a relative error of at most 0.015.
Values may be sent and summed in bfloat16 or wider, within the bound.
A program may use at most 64 MiB of HBM per device.

```python
import jax
import jax.numpy as jnp
from jax import lax

D = 5120
FF = 7168
TOK_DEV = 512
TOKENS = 4096
N_DEPTH = 8


def level_of(rng, shape, split, low, top_value):
    def one(axis_at, parts):
        draws = jax.random.uniform(jax.random.fold_in(jax.random.fold_in(rng, 6), axis_at), (parts,), jnp.float32, low / len(split), top_value / len(split))
        return jnp.repeat(jnp.exp(draws), shape[axis_at] // parts).reshape((-1,) + (1,) * (len(shape) - axis_at - 1))

    factor_of = one(*split[0])
    for cut in split[1:]:
        factor_of = factor_of * one(*cut)
    return factor_of


def noise(key, dims, width, bound, shards=(), dtype=jnp.bfloat16):
    result = width * jax.random.normal(key, dims, jnp.float32)
    if shards:
        result = result * level_of(key, dims, shards, -0.22, 0.18)
    return jnp.clip(result, -bound, bound).astype(dtype)


def setup_inputs(seed: int = 0) -> dict:
    seeds = jax.random.split(jax.random.key(seed), 6)
    layer_input = noise(seeds[0], (TOKENS, D), 1.0, 6.0, ((0, 8), (1, 8)))
    output_grad = noise(seeds[1], (TOKENS, D), 1.0, 6.0, ((0, 8), (1, 8)))
    w_gate = noise(seeds[2], (D, FF), D ** -0.5, 0.078125, ((0, 8), (1, 8)))
    w_up = noise(seeds[3], (D, FF), D ** -0.5, 0.078125, ((0, 8), (1, 8)))
    w_down = noise(seeds[4], (FF, D), FF ** -0.5, 0.0625, ((0, 8), (1, 8)))
    return dict(layer_input=layer_input, output_grad=output_grad, w_gate=w_gate, w_up=w_up, w_down=w_down)


def reference(layer_input, output_grad, w_gate, w_up, w_down):
    gate = jnp.dot(layer_input, w_gate, preferred_element_type=jnp.float32)
    up = jnp.dot(layer_input, w_up, preferred_element_type=jnp.float32)
    back = jnp.dot(output_grad, w_down.T, preferred_element_type=jnp.float32)
    sig = jax.nn.sigmoid(gate)
    silu = gate * sig
    act = (silu * up).astype(jnp.bfloat16)
    d_gate = (back * up * sig * (1.0 + gate * (1.0 - sig))).astype(jnp.bfloat16)
    d_up = (back * silu).astype(jnp.bfloat16)
    input_grad = (jnp.dot(d_gate, w_gate.T, preferred_element_type=jnp.float32)
                  + jnp.dot(d_up, w_up.T, preferred_element_type=jnp.float32))
    factor = float(TOKENS) ** -0.5
    total_gate = jnp.zeros((D, FF), jnp.float32)
    total_up = jnp.zeros((D, FF), jnp.float32)
    total_down = jnp.zeros((FF, D), jnp.float32)
    for block in range(N_DEPTH):
        lo = block * TOK_DEV
        x_blk = layer_input[lo:lo + TOK_DEV]
        g_blk = output_grad[lo:lo + TOK_DEV]
        term_gate = (jnp.dot(x_blk.T, d_gate[lo:lo + TOK_DEV], preferred_element_type=jnp.float32) * factor).astype(jnp.bfloat16)
        term_up = (jnp.dot(x_blk.T, d_up[lo:lo + TOK_DEV], preferred_element_type=jnp.float32) * factor).astype(jnp.bfloat16)
        term_down = (jnp.dot(act[lo:lo + TOK_DEV].T, g_blk, preferred_element_type=jnp.float32) * factor).astype(jnp.bfloat16)
        term_gate, term_up, term_down = lax.optimization_barrier((term_gate, term_up, term_down))
        total_gate = total_gate + term_gate.astype(jnp.float32)
        total_up = total_up + term_up.astype(jnp.float32)
        total_down = total_down + term_down.astype(jnp.float32)
    return (input_grad, total_gate, total_up, total_down)
```

```python
import jax
import jax.numpy as jnp
from jax import lax
from jax.experimental import pallas as pl
from jax.experimental.pallas import tpu as pltpu
from jax.sharding import PartitionSpec as P

MESH = pl.DeviceIdType.MESH
BF, F32 = jnp.bfloat16, jnp.float32

NY, NX, NZ = 4, 4, 8
TOK, FEAT, HID = 512, 640, 896
HALF = TOK // 2
QUART = HALF // NY
XTOK = TOK // NX
CHUNK = FEAT // NZ
ROWS = 3 * CHUNK
LANE = 128
UNITS = HID // LANE
SLICES = ((0, 256), (256, 256), (512, 256), (768, 128))
NS = len(SLICES)
HOPS = NZ - 1
STEPS = UNITS * HOPS
SKEW = 4


def swiglu_back(gate, up, back):
    sig = jax.nn.sigmoid(gate)
    silu = gate * sig
    d_gate = (back * up * sig * (1.0 + gate * (1.0 - sig))).astype(BF)
    return d_gate, (back * silu).astype(BF), (silu * up).astype(BF)


def dot(a, b):
    return jnp.dot(a, b, preferred_element_type=F32)


def dot_last(a, b):
    return lax.dot_general(a, b, (((1,), (1,)), ((), ())), preferred_element_type=F32)


def kernel(factor, x_ref, g_ref, wg_ref, wu_ref, wd_ref, ig_ref, wgr_ref, *scratch):
    it = iter(scratch)
    xt = next(it)
    ph = [next(it) for _ in SLICES]
    csend = [next(it) for _ in SLICES]
    crecv = [next(it) for _ in SLICES]
    ysend = [next(it) for _ in SLICES]
    yrecv = [next(it) for _ in SLICES]
    dbuf = [next(it) for _ in SLICES]
    zterm, zl, zr = next(it), next(it), next(it)
    ig, xsend, xrecv, hsend, hrecv, agbuf = (next(it) for _ in range(6))
    cs, cr, ys, yr, gs, gr, fs, fr, zs, zlr, zrr, xs, xr, hs, hr, ags, agr = it

    row, col, dep = lax.axis_index("row"), lax.axis_index("col"), lax.axis_index("depth")
    y, k = row // 2, row % 2
    x, zh = col // 2, col % 2
    other = (y * 2 + 1 - k, col, dep)

    def at_y(o):
        return (((y + o) % NY) * 2 + k, col, dep)

    def at_x(o):
        return (row, ((x + o) % NX) * 2 + zh, dep)

    partner = (row, x * 2 + 1 - zh, dep)
    up_z = (row, col, dep + 1)
    down_z = (row, col, dep - 1)

    barrier = pltpu.get_barrier_semaphore()

    def greet(dev):
        pl.semaphore_signal(barrier, inc=1, device_id=dev, device_id_type=MESH)

    for o in (1, 2, 3):
        greet(at_y(o))
        greet(at_x(o))
    greet(other)
    greet(partner)

    @pl.when(dep > 0)
    def _():
        greet(down_z)

    @pl.when(dep < NZ - 1)
    def _():
        greet(up_z)

    def copy(src, dst, ssem, rsem, dev):
        return pltpu.make_async_remote_copy(
            src_ref=src, dst_ref=dst, send_sem=ssem, recv_sem=rsem, device_id=dev, device_id_type=MESH
        )

    def partials(half, s):
        lo, w = SLICES[s]
        rows = pl.ds(pl.multiple_of(half * HALF, HALF), HALF)
        return (
            dot(x_ref[rows, :], wg_ref[:, lo:lo + w]),
            dot(x_ref[rows, :], wu_ref[:, lo:lo + w]),
            dot_last(g_ref[rows, :], wd_ref[lo:lo + w, :]),
        )

    def core_copy(s):
        return copy(csend[s], crecv[s], cs.at[s], cr.at[s], other)

    def first(s):
        for m, part in enumerate(partials(1 - k, s)):
            csend[s][m] = part.astype(BF)
        if s == 0:
            inner = jnp.where((dep > 0) & (dep < NZ - 1), 10, 9)
            pl.semaphore_wait(barrier, inner)
        core_copy(s).start()
        for m, part in enumerate(partials(k, s)):
            ph[s][m] = part

    def y_copy(s, o):
        return copy(ysend[s].at[(y + o) % NY], yrecv[s].at[o - 1], ys.at[s, o - 1], yr.at[s, o - 1], at_y(o))

    def reduce_core(s):
        core_copy(s).wait_recv()
        for m in range(3):
            total = ph[s][m] + crecv[s][m].astype(F32)
            ph[s][m] = total
            for b in range(NY):
                ysend[s][b, m] = total[b * QUART:(b + 1) * QUART].astype(BF)
        for o in (2, 1, 3):
            y_copy(s, o).start()

    def gather_copy(s, o):
        blk = k * NY + y
        return copy(dbuf[s].at[blk], dbuf[s].at[blk], gs.at[s, o - 1], gr.at[s, o - 1], at_y(o))

    def cross_copy(s, o):
        blk = k * NY + (y - o + NY) % NY
        return copy(dbuf[s].at[blk], dbuf[s].at[blk], fs.at[s, o], fr.at[s, o], other)

    def middle(s):
        for o in (1, 2, 3):
            y_copy(s, o).wait_recv()
        own = pl.ds(pl.multiple_of(y * QUART, QUART), QUART)
        sums = []
        for m in range(3):
            total = ph[s][m, own, :]
            for o in range(3):
                total = total + yrecv[s][o, m].astype(F32)
            sums.append(total)
        blk = k * NY + y
        for m, value in enumerate(swiglu_back(*sums)):
            dbuf[s][blk, m] = value
        for o in (2, 1, 3):
            gather_copy(s, o).start()
        cross_copy(s, 0).start()

    def spread(s):
        for o in (1, 3, 2):
            gather_copy(s, o).wait_recv()
            cross_copy(s, o).start()

    def arrive(s):
        for o in range(NY):
            cross_copy(s, o).wait_recv()

    def hidden(s, m):
        return dbuf[s][:, m].reshape(TOK, SLICES[s][1])

    def inputs(s):
        lo, w = SLICES[s]
        part = dot_last(hidden(s, 0), wg_ref[:, lo:lo + w]) + dot_last(hidden(s, 1), wu_ref[:, lo:lo + w])
        if s == 0:
            ig[...] = part
        elif s < NS - 1:
            ig[...] += part
        else:
            total = ig[...] + part
            ig[...] = total
            for b in range(NX):
                xsend[b] = total[b * XTOK:(b + 1) * XTOK].astype(BF)

    def weights(s):
        lo, w = SLICES[s]
        for m in range(3):
            term = (dot(xt[m // 2], hidden(s, m)) * factor).astype(BF)
            for v in range(w // LANE):
                for j in range(NZ):
                    zterm[lo // LANE + v, j, m * CHUNK:(m + 1) * CHUNK, :] = term[
                        j * CHUNK:(j + 1) * CHUNK, v * LANE:(v + 1) * LANE
                    ]

    def z_up(u, j):
        return copy(zterm.at[u, j], zl.at[u, j], zs.at[u, j], zlr.at[u, j], up_z)

    def z_down(u, j):
        return copy(zterm.at[u, j], zr.at[u, j], zs.at[u, j], zrr.at[u, j], down_z)

    def z_step(t, carry):
        q = t - SKEW * dep
        qc = jnp.clip(q, 0, STEPS - 1)
        u, j = qc // HOPS, HOPS - qc % HOPS

        @pl.when((q >= 0) & (q < STEPS) & (j > dep))
        def _():
            @pl.when(dep > 0)
            def _():
                z_up(u, j).wait_recv()
                zterm[u, j] = (zterm[u, j].astype(F32) + zl[u, j].astype(F32)).astype(BF)

            z_up(u, j).start()

        p = t - SKEW * (NZ - 1 - dep)
        pc = jnp.clip(p, 0, STEPS - 1)
        v, i = pc // HOPS, pc % HOPS

        @pl.when((p >= 0) & (p < STEPS) & (i < dep))
        def _():
            @pl.when(dep < NZ - 1)
            def _():
                z_down(v, i).wait_recv()
                zterm[v, i] = (zterm[v, i].astype(F32) + zr[v, i].astype(F32)).astype(BF)

            z_down(v, i).start()

        return carry

    def z_steps(lo, hi):
        lax.fori_loop(lo, hi, z_step, 0)

    def x_copy(o):
        return copy(xsend.at[(x + o) % NX], xrecv.at[o - 1], xs.at[o - 1], xr.at[o - 1], at_x(o))

    def hi_copy():
        return copy(hsend, hrecv, hs.at[0], hr.at[0], partner)

    def ag_copy(o):
        return copy(agbuf.at[x], agbuf.at[x], ags.at[o - 1], agr.at[o - 1], at_x(o))

    def units_of(s):
        lo, w = SLICES[s]
        return lo // LANE * HOPS, (lo + w) // LANE * HOPS

    for s in range(NS):
        first(s)
        if s > 0:
            reduce_core(s - 1)
    reduce_core(NS - 1)
    xt[0] = x_ref[...].T
    xt[1] = g_ref[...].T
    middle(0)
    middle(1)
    spread(0)
    middle(2)
    spread(1)
    arrive(0)
    inputs(0)
    weights(0)
    z_steps(*units_of(0))
    middle(3)
    spread(2)
    arrive(1)
    inputs(1)
    weights(1)
    z_steps(*units_of(1))
    spread(3)
    arrive(2)
    inputs(2)
    weights(2)
    z_steps(units_of(2)[0], units_of(2)[0] + HOPS)
    arrive(3)
    inputs(3)
    for o in (2, 1, 3):
        x_copy(o).start()
    weights(3)
    z_steps(units_of(2)[0] + HOPS, units_of(3)[0])
    for o in (1, 3, 2):
        x_copy(o).wait_recv()
    mine = pl.ds(pl.multiple_of(x * XTOK, XTOK), XTOK)
    total = ig[mine, :]
    for o in range(3):
        total = total + xrecv[o].astype(F32)
    hsend[...] = total.astype(BF)
    hi_copy().start()
    z_steps(units_of(3)[0], STEPS + SKEW * 2)
    hi_copy().wait_recv()
    agbuf[x] = (hsend[...].astype(F32) + hrecv[...].astype(F32)).astype(BF)
    for o in (2, 1, 3):
        ag_copy(o).start()
    z_steps(STEPS + SKEW * 2, STEPS + SKEW * (NZ - 1))

    def finish(u, carry):
        @pl.when(dep > 0)
        def _():
            z_up(u, dep).wait_recv()

        @pl.when(dep < NZ - 1)
        def _():
            z_down(u, dep).wait_recv()

        lanes = pl.ds(pl.multiple_of(u * LANE, LANE), LANE)
        wgr_ref[:, lanes] = zterm[u, dep].astype(F32)

        @pl.when(dep > 0)
        def _():
            wgr_ref[:, lanes] += zl[u, dep].astype(F32)

        @pl.when(dep < NZ - 1)
        def _():
            wgr_ref[:, lanes] += zr[u, dep].astype(F32)

        return carry

    lax.fori_loop(0, UNITS, finish, 0)

    for o in (1, 3, 2):
        ag_copy(o).wait_recv()
    ig_ref[...] = agbuf[...].reshape(TOK, FEAT)

    for s in range(NS):
        core_copy(s).wait_send()
        for o in (1, 2, 3):
            y_copy(s, o).wait_send()
            gather_copy(s, o).wait_send()
        for o in range(NY):
            cross_copy(s, o).wait_send()
    for o in (1, 2, 3):
        x_copy(o).wait_send()
        ag_copy(o).wait_send()
    hi_copy().wait_send()

    def drain(q, carry):
        u, j = q // NZ, q % NZ

        @pl.when(j != dep)
        def _():
            z_up(u, j).wait_send()

        return carry

    lax.fori_loop(0, UNITS * NZ, drain, 0)


def shards(layer_input, output_grad, w_gate, w_up, w_down):
    factor = float(layer_input.shape[0] * lax.axis_size("depth")) ** (-0.5)
    dma = pltpu.SemaphoreType.DMA

    def per_slice(lead, dtype):
        return [pltpu.VMEM((*lead, w), dtype) for _, w in SLICES]

    scratch = [
        pltpu.VMEM((2, FEAT, TOK), BF),
        *per_slice((3, HALF), F32),
        *per_slice((3, HALF), BF),
        *per_slice((3, HALF), BF),
        *per_slice((NY, 3, QUART), BF),
        *per_slice((NY - 1, 3, QUART), BF),
        *per_slice((2 * NY, 3, QUART), BF),
        pltpu.VMEM((UNITS, NZ, ROWS, LANE), BF),
        pltpu.VMEM((UNITS, NZ, ROWS, LANE), BF),
        pltpu.VMEM((UNITS, NZ, ROWS, LANE), BF),
        pltpu.VMEM((TOK, FEAT), F32),
        pltpu.VMEM((NX, XTOK, FEAT), BF),
        pltpu.VMEM((NX - 1, XTOK, FEAT), BF),
        pltpu.VMEM((XTOK, FEAT), BF),
        pltpu.VMEM((XTOK, FEAT), BF),
        pltpu.VMEM((NX, XTOK, FEAT), BF),
        dma((NS,)), dma((NS,)),
        dma((NS, 3)), dma((NS, 3)),
        dma((NS, 3)), dma((NS, 3)),
        dma((NS, NY)), dma((NS, NY)),
        dma((UNITS, NZ)), dma((UNITS, NZ)), dma((UNITS, NZ)),
        dma((3,)), dma((3,)),
        dma((1,)), dma((1,)),
        dma((3,)), dma((3,)),
    ]
    vmem = pl.BlockSpec(memory_space=pltpu.VMEM)
    ig, wgr = pl.pallas_call(
        lambda *refs: kernel(factor, *refs),
        out_shape=(
            jax.ShapeDtypeStruct((TOK, FEAT), BF),
            jax.ShapeDtypeStruct((ROWS, HID), F32),
        ),
        in_specs=[vmem] * 5,
        out_specs=(vmem, vmem),
        scratch_shapes=scratch,
        compiler_params=pltpu.CompilerParams(
            collective_id=0, has_side_effects=True, vmem_limit_bytes=56 * 2 ** 20
        ),
        name="swiglu_back",
    )(layer_input, output_grad, w_gate, w_up, w_down)
    return ig.astype(F32), wgr[:CHUNK], wgr[CHUNK:2 * CHUNK], wgr[2 * CHUNK:].T


def solution(mesh):
    in_specs = (
        P("depth", "row"),
        P("depth", "row"),
        P("row", "col"),
        P("row", "col"),
        P("col", "row"),
    )
    out_specs = (
        P("depth", "row"),
        P(("row", "depth"), "col"),
        P(("row", "depth"), "col"),
        P("col", ("row", "depth")),
    )
    return jax.shard_map(shards, mesh=mesh, in_specs=in_specs, out_specs=out_specs, check_vma=False)
```

```python
import jax
import jax.numpy as jnp
from jax import lax
from jax.experimental import pallas as pl
from jax.experimental.pallas import tpu as pltpu
from jax.sharding import PartitionSpec as P

MESH = pl.DeviceIdType.MESH
BF, F32 = jnp.bfloat16, jnp.float32

NY, NX, NZ = 4, 4, 8
TOK, FEAT, HID = 512, 640, 896
HALF = TOK // 2
QUART = HALF // NY
XTOK = TOK // NX
CHUNK = FEAT // NZ
ROWS = 3 * CHUNK
LANE = 128
UNITS = HID // LANE
SLICES = ((0, 128), (128, 256), (384, 256), (640, 256))
NS = len(SLICES)
HOPS = NZ - 1
STEPS = UNITS * HOPS
EARLY = 3
LATE = UNITS - EARLY
SKEW = 4
LAST = STEPS + SKEW * (NZ - 3)


def swiglu_back(gate, up, back):
    sig = jax.nn.sigmoid(gate)
    silu = gate * sig
    d_gate = (back * up * sig * (1.0 + gate * (1.0 - sig))).astype(BF)
    return d_gate, (back * silu).astype(BF), (silu * up).astype(BF)


def dot(a, b):
    return jnp.dot(a, b, preferred_element_type=F32)


def dot_last(a, b):
    return lax.dot_general(a, b, (((1,), (1,)), ((), ())), preferred_element_type=F32)


def kernel(factor, x_in, g_in, wg_in, wu_in, wd_in, ig_ref, wgr_ref, *scratch):
    it = iter(scratch)
    x_ref, g_ref, wg_ref, wu_ref, wd_ref, loads, ring = (next(it) for _ in range(7))
    load = [
        pltpu.make_async_copy(src, dst, loads.at[n])
        for n, (src, dst) in enumerate(
            ((x_in, x_ref), (wg_in, wg_ref), (wu_in, wu_ref), (g_in, g_ref), (wd_in, wd_ref))
        )
    ]
    for c in load:
        c.start()
    xt = next(it)
    ph = [next(it) for _ in SLICES]
    csend = [next(it) for _ in SLICES]
    crecv = [next(it) for _ in SLICES]
    ysend = [next(it) for _ in SLICES]
    yrecv = [next(it) for _ in SLICES]
    dbuf = [next(it) for _ in SLICES]
    zterm, zl, zr = next(it), next(it), next(it)
    ig, xsend, xrecv, hsend, hrecv, agbuf = (next(it) for _ in range(6))
    cs, cr, ys, yr, gs, gr, fs, fr, zs, zlr, zrr, xs, xr, hs, hr, ags, agr = it

    row, col, dep = lax.axis_index("row"), lax.axis_index("col"), lax.axis_index("depth")
    y, k = row // 2, row % 2
    x, zh = col // 2, col % 2
    other = (y * 2 + 1 - k, col, dep)

    def at_y(o):
        return (((y + o) % NY) * 2 + k, col, dep)

    def at_x(o):
        return (row, ((x + o) % NX) * 2 + zh, dep)

    partner = (row, x * 2 + 1 - zh, dep)
    up_z = (row, x * 2 + (zh + (dep + 1) // NZ) % 2, (dep + 1) % NZ)
    down_z = (row, x * 2 + (zh + 1 - (dep + NZ - 1) // NZ) % 2, (dep + NZ - 1) % NZ)

    barrier = pltpu.get_barrier_semaphore()
    near = [at_y(1), at_y(2), at_y(3), at_x(1), at_x(2), at_x(3), other, up_z, down_z]
    for dev in near:
        pl.semaphore_signal(barrier, inc=1, device_id=dev, device_id_type=MESH)

    def tell():
        pl.semaphore_signal(ring, inc=1, device_id=up_z, device_id_type=MESH)

    def pass_on():
        pl.semaphore_wait(ring, 1)
        tell()

    def copy(src, dst, ssem, rsem, dev):
        return pltpu.make_async_remote_copy(
            src_ref=src, dst_ref=dst, send_sem=ssem, recv_sem=rsem, device_id=dev, device_id_type=MESH
        )

    def partials(half, s, loaded):
        lo, w = SLICES[s]
        rows = pl.ds(pl.multiple_of(half * HALF, HALF), HALF)
        if not loaded:
            load[0].wait()
            load[1].wait()
        yield dot(x_ref[rows, :], wg_ref[:, lo:lo + w])
        if not loaded:
            load[2].wait()
        yield dot(x_ref[rows, :], wu_ref[:, lo:lo + w])
        if not loaded:
            load[3].wait()
            load[4].wait()
        yield dot_last(g_ref[rows, :], wd_ref[lo:lo + w, :])

    def core_copy(s):
        return copy(csend[s], crecv[s], cs.at[s], cr.at[s], other)

    def first(s):
        for m, part in enumerate(partials(1 - k, s, s > 0)):
            csend[s][m] = part.astype(BF)
        if s == 0:
            pl.semaphore_wait(barrier, len(near))
            tell()
        core_copy(s).start()
        for m, part in enumerate(partials(k, s, True)):
            ph[s][m] = part

    def y_copy(s, o):
        return copy(ysend[s].at[(y + o) % NY], yrecv[s].at[o - 1], ys.at[s, o - 1], yr.at[s, o - 1], at_y(o))

    def reduce_core(s):
        core_copy(s).wait_recv()
        for m in range(3):
            total = ph[s][m] + crecv[s][m].astype(F32)
            ph[s][m] = total
            for b in range(NY):
                ysend[s][b, m] = total[b * QUART:(b + 1) * QUART].astype(BF)
        for o in (2, 1, 3):
            y_copy(s, o).start()

    def gather_copy(s, o):
        blk = k * NY + y
        return copy(dbuf[s].at[blk], dbuf[s].at[blk], gs.at[s, o - 1], gr.at[s, o - 1], at_y(o))

    def cross_copy(s, o):
        blk = k * NY + (y - o + NY) % NY
        return copy(dbuf[s].at[blk], dbuf[s].at[blk], fs.at[s, o], fr.at[s, o], other)

    def middle(s):
        for o in (1, 2, 3):
            y_copy(s, o).wait_recv()
        own = pl.ds(pl.multiple_of(y * QUART, QUART), QUART)
        sums = []
        for m in range(3):
            total = ph[s][m, own, :]
            for o in range(3):
                total = total + yrecv[s][o, m].astype(F32)
            sums.append(total)
        blk = k * NY + y
        for m, value in enumerate(swiglu_back(*sums)):
            dbuf[s][blk, m] = value
        for o in (2, 1, 3):
            gather_copy(s, o).start()
        cross_copy(s, 0).start()

    def spread(s):
        for o in (1, 3, 2):
            gather_copy(s, o).wait_recv()
            cross_copy(s, o).start()

    def arrive(s):
        for o in range(NY):
            cross_copy(s, o).wait_recv()

    def hidden(s, m):
        return dbuf[s][:, m].reshape(TOK, SLICES[s][1])

    def inputs(s):
        lo, w = SLICES[s]
        part = dot_last(hidden(s, 0), wg_ref[:, lo:lo + w]) + dot_last(hidden(s, 1), wu_ref[:, lo:lo + w])
        if s == 0:
            ig[...] = part
        elif s < NS - 1:
            ig[...] += part
        else:
            total = ig[...] + part
            ig[...] = total
            for b in range(NX):
                xsend[b] = total[b * XTOK:(b + 1) * XTOK].astype(BF)

    def weights(s):
        lo, w = SLICES[s]
        for m in range(3):
            term = (dot(xt[m // 2], hidden(s, m)) * factor).astype(BF)
            for v in range(w // LANE):
                for j in range(NZ):
                    zterm[lo // LANE + v, j, m * CHUNK:(m + 1) * CHUNK, :] = term[
                        j * CHUNK:(j + 1) * CHUNK, v * LANE:(v + 1) * LANE
                    ]

    def z_up(u, j):
        return copy(zterm.at[u, j], zl.at[u, j], zs.at[u, j], zlr.at[u, j], up_z)

    def z_down(u, j):
        return copy(zterm.at[u, j], zr.at[u, j], zs.at[u, j], zrr.at[u, j], down_z)

    def place(q):
        late = q - EARLY * HOPS
        u = jnp.where(late < 0, q // HOPS, EARLY + late % LATE)
        return u, jnp.where(late < 0, q % HOPS, late // LATE)

    def z_first(lo, hi):
        def send(q, carry):
            u, j = place(q)

            @pl.when(dep == 0)
            def _():
                z_up(u, HOPS - j).start()

            @pl.when(dep == NZ - 1)
            def _():
                z_down(u, j).start()

            return carry

        lax.fori_loop(lo * HOPS, hi * HOPS, send, 0)

    def z_step(t, carry):
        q = t - SKEW * (dep - 1)
        u, j = place(jnp.clip(q, 0, STEPS - 1))
        j = HOPS - j

        @pl.when((q >= 0) & (q < STEPS) & (j > dep) & (dep > 0))
        def _():
            z_up(u, j).wait_recv()
            zterm[u, j] = (zterm[u, j].astype(F32) + zl[u, j].astype(F32)).astype(BF)
            z_up(u, j).start()

        p = t - SKEW * (NZ - 2 - dep)
        v, i = place(jnp.clip(p, 0, STEPS - 1))

        @pl.when((p >= 0) & (p < STEPS) & (i < dep) & (dep < NZ - 1))
        def _():
            z_down(v, i).wait_recv()
            zterm[v, i] = (zterm[v, i].astype(F32) + zr[v, i].astype(F32)).astype(BF)
            z_down(v, i).start()

        return carry

    def z_steps(lo, hi):
        lax.fori_loop(lo, hi, z_step, 0)

    def x_copy(o):
        return copy(xsend.at[(x + o) % NX], xrecv.at[o - 1], xs.at[o - 1], xr.at[o - 1], at_x(o))

    def hi_copy():
        return copy(hsend, hrecv, hs.at[0], hr.at[0], partner)

    def ag_copy(o):
        return copy(agbuf.at[x], agbuf.at[x], ags.at[o - 1], agr.at[o - 1], at_x(o))

    first(0)
    first(1)
    reduce_core(0)
    xt[0] = x_ref[...].T
    xt[1] = g_ref[...].T
    pass_on()
    first(2)
    middle(0)
    reduce_core(1)
    pass_on()
    first(3)
    reduce_core(2)
    spread(0)
    arrive(0)
    weights(0)
    z_first(0, 1)
    pass_on()
    middle(1)
    reduce_core(3)
    inputs(0)
    pass_on()
    spread(1)
    arrive(1)
    weights(1)
    z_first(1, EARLY)
    pass_on()
    middle(2)
    inputs(1)
    z_steps(0, 4)
    pass_on()
    middle(3)
    z_steps(4, 7)
    spread(2)
    arrive(2)
    inputs(2)
    pass_on()
    z_steps(7, 10)
    spread(3)
    arrive(3)
    inputs(3)
    for o in (2, 1, 3):
        x_copy(o).start()
    weights(2)
    weights(3)
    z_first(EARLY, UNITS)
    z_steps(10, 20)
    for o in (1, 3, 2):
        x_copy(o).wait_recv()
    mine = pl.ds(pl.multiple_of(x * XTOK, XTOK), XTOK)
    total = ig[mine, :]
    for o in range(3):
        total = total + xrecv[o].astype(F32)
    hsend[...] = total.astype(BF)
    pl.semaphore_wait(ring, 1)
    hi_copy().start()
    z_steps(20, 36)
    hi_copy().wait_recv()
    agbuf[x] = (hsend[...].astype(F32) + hrecv[...].astype(F32)).astype(BF)
    for o in (2, 1, 3):
        ag_copy(o).start()
    z_steps(36, LAST)

    def finish(u, carry):
        @pl.when(dep > 0)
        def _():
            z_up(u, dep).wait_recv()

        @pl.when(dep < NZ - 1)
        def _():
            z_down(u, dep).wait_recv()

        lanes = pl.ds(pl.multiple_of(u * LANE, LANE), LANE)
        wgr_ref[:, lanes] = zterm[u, dep].astype(F32)

        @pl.when(dep > 0)
        def _():
            wgr_ref[:, lanes] += zl[u, dep].astype(F32)

        @pl.when(dep < NZ - 1)
        def _():
            wgr_ref[:, lanes] += zr[u, dep].astype(F32)

        return carry

    lax.fori_loop(0, UNITS, finish, 0)

    for o in (1, 3, 2):
        ag_copy(o).wait_recv()
    ig_ref[...] = agbuf[...].reshape(TOK, FEAT)

    for s in range(NS):
        core_copy(s).wait_send()
        for o in (1, 2, 3):
            y_copy(s, o).wait_send()
            gather_copy(s, o).wait_send()
        for o in range(NY):
            cross_copy(s, o).wait_send()
    for o in (1, 2, 3):
        x_copy(o).wait_send()
        ag_copy(o).wait_send()
    hi_copy().wait_send()

    def drain(q, carry):
        u, j = q // NZ, q % NZ

        @pl.when(j != dep)
        def _():
            z_up(u, j).wait_send()

        return carry

    lax.fori_loop(0, UNITS * NZ, drain, 0)


def shards(layer_input, output_grad, w_gate, w_up, w_down):
    factor = float(layer_input.shape[0] * lax.axis_size("depth")) ** (-0.5)
    dma = pltpu.SemaphoreType.DMA

    def per_slice(lead, dtype):
        return [pltpu.VMEM((*lead, w), dtype) for _, w in SLICES]

    scratch = [
        pltpu.VMEM((TOK, FEAT), BF),
        pltpu.VMEM((TOK, FEAT), BF),
        pltpu.VMEM((FEAT, HID), BF),
        pltpu.VMEM((FEAT, HID), BF),
        pltpu.VMEM((HID, FEAT), BF),
        dma((5,)),
        pltpu.SemaphoreType.REGULAR,
        pltpu.VMEM((2, FEAT, TOK), BF),
        *per_slice((3, HALF), F32),
        *per_slice((3, HALF), BF),
        *per_slice((3, HALF), BF),
        *per_slice((NY, 3, QUART), BF),
        *per_slice((NY - 1, 3, QUART), BF),
        *per_slice((2 * NY, 3, QUART), BF),
        pltpu.VMEM((UNITS, NZ, ROWS, LANE), BF),
        pltpu.VMEM((UNITS, NZ, ROWS, LANE), BF),
        pltpu.VMEM((UNITS, NZ, ROWS, LANE), BF),
        pltpu.VMEM((TOK, FEAT), F32),
        pltpu.VMEM((NX, XTOK, FEAT), BF),
        pltpu.VMEM((NX - 1, XTOK, FEAT), BF),
        pltpu.VMEM((XTOK, FEAT), BF),
        pltpu.VMEM((XTOK, FEAT), BF),
        pltpu.VMEM((NX, XTOK, FEAT), BF),
        dma((NS,)), dma((NS,)),
        dma((NS, 3)), dma((NS, 3)),
        dma((NS, 3)), dma((NS, 3)),
        dma((NS, NY)), dma((NS, NY)),
        dma((UNITS, NZ)), dma((UNITS, NZ)), dma((UNITS, NZ)),
        dma((3,)), dma((3,)),
        dma((1,)), dma((1,)),
        dma((3,)), dma((3,)),
    ]
    vmem = pl.BlockSpec(memory_space=pltpu.VMEM)
    ig, wgr = pl.pallas_call(
        lambda *refs: kernel(factor, *refs),
        out_shape=(
            jax.ShapeDtypeStruct((TOK, FEAT), BF),
            jax.ShapeDtypeStruct((ROWS, HID), F32),
        ),
        in_specs=[pl.BlockSpec(memory_space=pl.ANY)] * 5,
        out_specs=(vmem, vmem),
        scratch_shapes=scratch,
        compiler_params=pltpu.CompilerParams(
            collective_id=0, has_side_effects=True, vmem_limit_bytes=56 * 2 ** 20
        ),
        name="swiglu_back",
    )(layer_input, output_grad, w_gate, w_up, w_down)
    return ig.astype(F32), wgr[:CHUNK], wgr[CHUNK:2 * CHUNK], wgr[2 * CHUNK:].T


def solution(mesh):
    in_specs = (
        P("depth", "row"),
        P("depth", "row"),
        P("row", "col"),
        P("row", "col"),
        P("col", "row"),
    )
    out_specs = (
        P("depth", "row"),
        P(("row", "depth"), "col"),
        P(("row", "depth"), "col"),
        P("col", ("row", "depth")),
    )
    return jax.shard_map(shards, mesh=mesh, in_specs=in_specs, out_specs=out_specs, check_vma=False)
```

```python
import jax
import jax.numpy as jnp
from jax import lax
from jax.experimental import pallas as pl
from jax.experimental.pallas import tpu as pltpu
from jax.sharding import PartitionSpec as P

MESH = pl.DeviceIdType.MESH
BF, F32 = jnp.bfloat16, jnp.float32

NY, NX, NZ = 4, 4, 8
TOK, FEAT, HID = 512, 640, 896
HALF = TOK // 2
QUART = HALF // NY
XTOK = TOK // NX
CHUNK = FEAT // NZ
ROWS = 3 * CHUNK
LANE = 128
UNITS = HID // LANE
SLICES = ((0, 128), (128, 128), (256, 256), (512, 384))
NS = len(SLICES)
HOPS = NZ - 1
EARLY = 4
LATE = UNITS - EARLY
MOVED = (3,)
NM = len(MOVED)
SKEW = 4
FAR = HOPS - 2
FIRST = HOPS
SECOND = FIRST + FAR
THIRD = SECOND + (EARLY - 2) * FAR
NEAR_STEPS = EARLY * HOPS
FAR_STEPS = THIRD + LATE * FAR
LAST = THIRD + max(LATE * (HOPS - d) + SKEW * (d - 1) for d in range(2, HOPS))


def swiglu_back(gate, up, back):
    sig = jax.nn.sigmoid(gate)
    silu = gate * sig
    d_gate = (back * up * sig * (1.0 + gate * (1.0 - sig))).astype(BF)
    return d_gate, (back * silu).astype(BF), (silu * up).astype(BF)


def dot(a, b):
    return jnp.dot(a, b, preferred_element_type=F32)


def dot_last(a, b):
    return lax.dot_general(a, b, (((1,), (1,)), ((), ())), preferred_element_type=F32)


def kernel(factor, x_in, g_in, wg_in, wu_in, wd_in, ig_ref, wgr_ref, *scratch):
    it = iter(scratch)
    x_ref, g_ref, wg_ref, wu_ref, wd_ref, loads, ring = (next(it) for _ in range(7))
    load = [
        pltpu.make_async_copy(src, dst, loads.at[n])
        for n, (src, dst) in enumerate(
            ((x_in, x_ref), (wg_in, wg_ref), (wu_in, wu_ref), (g_in, g_ref), (wd_in, wd_ref))
        )
    ]
    for c in load:
        c.start()
    xt = next(it)
    ph = [next(it) for _ in SLICES]
    csend = [next(it) for _ in SLICES]
    crecv = [next(it) for _ in SLICES]
    ysend = [next(it) for _ in SLICES]
    yrecv = [next(it) for _ in SLICES]
    dbuf = [next(it) for _ in SLICES]
    zterm, zl, zr = next(it), next(it), next(it)
    ig, xsend, xrecv, hsend, hrecv, agbuf = (next(it) for _ in range(6))
    ownq, fq, xt2, fsum = next(it), next(it), next(it), next(it)
    fd = [next(it) for _ in MOVED]
    cs, cr, ys, yr, gs, gr, fs, fr, zs, zlr, zrr, xs, xr, hs, hr, ags, agr, *it = it
    qs, qr, ds, dr, fxs, fxr, fgs, fgr, ffs, ffr = it

    row, col, dep = lax.axis_index("row"), lax.axis_index("col"), lax.axis_index("depth")
    y, k = row // 2, row % 2
    x, zh = col // 2, col % 2
    other = (y * 2 + 1 - k, col, dep)

    def at_y(o):
        return (((y + o) % NY) * 2 + k, col, dep)

    def at_x(o):
        return (row, ((x + o) % NX) * 2 + zh, dep)

    partner = (row, x * 2 + 1 - zh, dep)
    up_z = (row, x * 2 + (zh + (dep + 1) // NZ) % 2, (dep + 1) % NZ)
    down_z = (row, x * 2 + (zh + 1 - (dep + NZ - 1) // NZ) % 2, (dep + NZ - 1) % NZ)

    barrier = pltpu.get_barrier_semaphore()
    near = [at_y(1), at_y(2), at_y(3), at_x(1), at_x(2), at_x(3), other, up_z, down_z]
    for dev in near:
        pl.semaphore_signal(barrier, inc=1, device_id=dev, device_id_type=MESH)

    left = dep < NZ // 2
    rank = jnp.where(left, dep, NZ - 1 - dep)
    inward = (row, col, jnp.where(left, dep + 1, dep - 1))
    blk = k * NY + y

    def tell():
        pl.semaphore_signal(ring, inc=1, device_id=up_z, device_id_type=MESH)

    def pass_on():
        pl.semaphore_wait(ring, 1)
        tell()

    def copy(src, dst, ssem, rsem, dev):
        return pltpu.make_async_remote_copy(
            src_ref=src, dst_ref=dst, send_sem=ssem, recv_sem=rsem, device_id=dev, device_id_type=MESH
        )

    def partials(half, s, loaded):
        lo, w = SLICES[s]
        rows = pl.ds(pl.multiple_of(half * HALF, HALF), HALF)
        if not loaded:
            load[0].wait()
            load[1].wait()
        yield dot(x_ref[rows, :], wg_ref[:, lo:lo + w])
        if not loaded:
            load[2].wait()
        yield dot(x_ref[rows, :], wu_ref[:, lo:lo + w])
        if not loaded:
            load[3].wait()
            load[4].wait()
        yield dot_last(g_ref[rows, :], wd_ref[lo:lo + w, :])

    def core_copy(s):
        return copy(csend[s], crecv[s], cs.at[s], cr.at[s], other)

    def first(s):
        for m, part in enumerate(partials(1 - k, s, s > 0)):
            csend[s][m] = part.astype(BF)
        if s == 0:
            pl.semaphore_wait(barrier, len(near))
            tell()
        core_copy(s).start()
        for m, part in enumerate(partials(k, s, True)):
            ph[s][m] = part

    def y_copy(s, o):
        return copy(ysend[s].at[(y + o) % NY], yrecv[s].at[o - 1], ys.at[s, o - 1], yr.at[s, o - 1], at_y(o))

    def reduce_core(s):
        core_copy(s).wait_recv()
        for m in range(3):
            total = ph[s][m] + crecv[s][m].astype(F32)
            ph[s][m] = total
            for b in range(NY):
                ysend[s][b, m] = total[b * QUART:(b + 1) * QUART].astype(BF)
        for o in (2, 1, 3):
            y_copy(s, o).start()

    def gather_copy(s, o):
        return copy(dbuf[s].at[blk], dbuf[s].at[blk], gs.at[s, o - 1], gr.at[s, o - 1], at_y(o))

    def cross_copy(s, o):
        b = k * NY + (y - o + NY) % NY
        return copy(dbuf[s].at[b], dbuf[s].at[b], fs.at[s, o], fr.at[s, o], other)

    def middle(s):
        for o in (1, 2, 3):
            y_copy(s, o).wait_recv()
        own = pl.ds(pl.multiple_of(y * QUART, QUART), QUART)
        sums = []
        for m in range(3):
            total = ph[s][m, own, :]
            for o in range(3):
                total = total + yrecv[s][o, m].astype(F32)
            sums.append(total)
        for m, value in enumerate(swiglu_back(*sums)):
            dbuf[s][blk, m] = value
        for o in (2, 1, 3):
            gather_copy(s, o).start()
        cross_copy(s, 0).start()

    def spread(s):
        for o in (1, 3, 2):
            gather_copy(s, o).wait_recv()
            cross_copy(s, o).start()

    def arrive(s):
        for o in range(NY):
            cross_copy(s, o).wait_recv()

    def hidden(s, m):
        return dbuf[s][:, m].reshape(TOK, SLICES[s][1])

    def inputs(s):
        lo, w = SLICES[s]
        part = dot_last(hidden(s, 0), wg_ref[:, lo:lo + w]) + dot_last(hidden(s, 1), wu_ref[:, lo:lo + w])
        if s == 0:
            ig[...] = part
        elif s < NS - 1:
            ig[...] += part
        else:
            total = ig[...] + part
            ig[...] = total
            for b in range(NX):
                xsend[b] = total[b * XTOK:(b + 1) * XTOK].astype(BF)

    def weights(s):
        lo, w = SLICES[s]
        for m in range(3):
            term = (dot(xt[m // 2], hidden(s, m)) * factor).astype(BF)
            for v in range(w // LANE):
                for j in range(NZ):
                    zterm[lo // LANE + v, j, m * CHUNK:(m + 1) * CHUNK, :] = term[
                        j * CHUNK:(j + 1) * CHUNK, v * LANE:(v + 1) * LANE
                    ]

    def z_up(u, j):
        return copy(zterm.at[u, j], zl.at[u, j], zs.at[u, j], zlr.at[u, j], up_z)

    def z_down(u, j):
        return copy(zterm.at[u, j], zr.at[u, j], zs.at[u, j], zrr.at[u, j], down_z)

    def z_first(lo, hi):
        def send(q, carry):
            _, u, n = place(q, False)

            @pl.when(dep == 0)
            def _():
                z_up(u, HOPS - n).start()

            @pl.when(dep == NZ - 1)
            def _():
                z_down(u, n).start()

            return carry

        lax.fori_loop(lo, hi, send, 0)

    def forward_up(u, j, waits):
        @pl.when(waits)
        def _():
            z_up(u, j).wait_recv()
            zterm[u, j] = (zterm[u, j].astype(F32) + zl[u, j].astype(F32)).astype(BF)

        z_up(u, j).start()

    def forward_down(u, j, waits):
        @pl.when(waits)
        def _():
            z_down(u, j).wait_recv()
            zterm[u, j] = (zterm[u, j].astype(F32) + zr[u, j].astype(F32)).astype(BF)

        z_down(u, j).start()

    def place(q, far):
        late = far & (q >= THIRD)
        r2, r3 = jnp.maximum(q - SECOND, 0), jnp.maximum(q - THIRD, 0)
        u = jnp.where(late, EARLY + r3 % LATE, 1 + r3 % (EARLY - 1))
        u = jnp.where(q < THIRD, 2 + r2 % (EARLY - 2), u)
        u = jnp.where(q < SECOND, jnp.where(q < FIRST, 0, 1), u)
        n = jnp.where(late, r3 // LATE, FAR + r3 // (EARLY - 1))
        n = jnp.where(q < THIRD, r2 // (EARLY - 2), n)
        n = jnp.where(q < SECOND, jnp.where(q < FIRST, q, q - FIRST), n)
        return late, u, n

    def z_step(t, carry):
        q = t - SKEW * (dep - 1)
        end = jnp.where(dep >= 2, FAR_STEPS, NEAR_STEPS)
        late, u, j = place(jnp.clip(q, 0, end - 1), dep >= 2)
        j = HOPS - j

        @pl.when((q >= 0) & (q < end) & (j > dep) & (dep > 0))
        def _():
            forward_up(u, j, dep > jnp.where(late, 2, 0))

        p = t - SKEW * (NZ - 2 - dep)
        end = jnp.where(dep <= NZ - 3, FAR_STEPS, NEAR_STEPS)
        late, v, i = place(jnp.clip(p, 0, end - 1), dep <= NZ - 3)

        @pl.when((p >= 0) & (p < end) & (i < dep) & (dep < NZ - 1))
        def _():
            forward_down(v, i, dep < jnp.where(late, NZ - 3, NZ - 1))

        return carry

    def z_steps(lo, hi):
        lax.fori_loop(lo, hi, z_step, 0)

    def q_copy(slot, src):
        return copy(src, fq.at[slot, x], qs.at[slot], qr.at[slot], inward)

    def d_copy(n, slot, src):
        return copy(src, fd[n].at[slot, blk], ds.at[n, slot], dr.at[n, slot], inward)

    def fx_copy(slot, o):
        return copy(fq.at[slot, x], fq.at[slot, x], fxs.at[slot, o - 1], fxr.at[slot, o - 1], at_x(o))

    def fg_copy(n, slot, o):
        return copy(
            fd[n].at[slot, blk], fd[n].at[slot, blk], fgs.at[n, slot, o - 1], fgr.at[n, slot, o - 1], at_y(o)
        )

    def ff_copy(n, slot, o):
        b = k * NY + (y - o + NY) % NY
        return copy(fd[n].at[slot, b], fd[n].at[slot, b], ffs.at[n, slot, o], ffr.at[n, slot, o], other)

    def send_q():
        @pl.when(rank < 2)
        def _():
            part = pl.ds(pl.multiple_of(x * XTOK, XTOK), XTOK)
            ownq[0] = x_ref[part, :]
            ownq[1] = g_ref[part, :]
            q_copy(rank, ownq).start()

    def relay_q():
        @pl.when(rank == 1)
        def _():
            q_copy(0, fq.at[0, x]).wait_recv()
            q_copy(0, fq.at[0, x]).start()

    def collect_q(slot):
        @pl.when(rank == 2)
        def _():
            q_copy(slot, ownq).wait_recv()
            for o in (2, 1, 3):
                fx_copy(slot, o).start()

    def turn_q(slot):
        @pl.when(rank == 2)
        def _():
            for o in (1, 3, 2):
                fx_copy(slot, o).wait_recv()
            for m in range(2):
                xt2[slot, m] = fq[slot, :, m].reshape(TOK, FEAT).T

    def send_d(n):
        @pl.when(rank < 2)
        def _():
            d_copy(n, rank, dbuf[MOVED[n]].at[blk]).start()

    def relay_d(n):
        @pl.when(rank == 1)
        def _():
            d_copy(n, 0, fd[n].at[0, blk]).wait_recv()
            d_copy(n, 0, fd[n].at[0, blk]).start()

    def collect_d(n, slot):
        @pl.when(rank == 2)
        def _():
            d_copy(n, slot, fd[n].at[slot, blk]).wait_recv()
            for o in (2, 1, 3):
                fg_copy(n, slot, o).start()
            ff_copy(n, slot, 0).start()

    def spread_d(n, slot):
        @pl.when(rank == 2)
        def _():
            for o in (1, 3, 2):
                fg_copy(n, slot, o).wait_recv()
                ff_copy(n, slot, o).start()

    def add_d(n):
        @pl.when(rank == 2)
        def _():
            lo, w = SLICES[MOVED[n]]
            for slot in range(2):
                for o in range(NY):
                    ff_copy(n, slot, o).wait_recv()
                for m in range(3):
                    term = dot(xt2[slot, m // 2], fd[n][slot, :, m].reshape(TOK, w)) * factor
                    for j in range(NZ):
                        counts = jnp.where(left, j, NZ - 1 - j) > slot
                        for v in range(w // LANE):
                            u = lo // LANE + v
                            rows = slice(m * CHUNK, (m + 1) * CHUNK)
                            more = term[j * CHUNK:(j + 1) * CHUNK, v * LANE:(v + 1) * LANE]
                            fsum[u - EARLY, j, rows, :] = (
                                fsum[u - EARLY, j, rows, :] + jnp.where(counts, more, 0.0)
                                if slot else jnp.where(counts, more, 0.0)
                            )
                            if slot:
                                zterm[u, j, rows, :] = (
                                    zterm[u, j, rows, :].astype(F32) + fsum[u - EARLY, j, rows, :]
                                ).astype(BF)

    def x_copy(o):
        return copy(xsend.at[(x + o) % NX], xrecv.at[o - 1], xs.at[o - 1], xr.at[o - 1], at_x(o))

    def hi_copy():
        return copy(hsend, hrecv, hs.at[0], hr.at[0], partner)

    def ag_copy(o):
        return copy(agbuf.at[x], agbuf.at[x], ags.at[o - 1], agr.at[o - 1], at_x(o))

    first(0)
    send_q()
    first(1)
    reduce_core(0)
    xt[0] = x_ref[...].T
    xt[1] = g_ref[...].T
    pass_on()
    first(2)
    middle(0)
    reduce_core(1)
    pass_on()
    first(3)
    reduce_core(2)
    relay_q()
    spread(0)
    arrive(0)
    weights(0)
    z_first(0, FIRST)
    collect_q(1)
    pass_on()
    middle(1)
    reduce_core(3)
    inputs(0)
    pass_on()
    spread(1)
    arrive(1)
    weights(1)
    z_first(FIRST, SECOND)
    collect_q(0)
    pass_on()
    middle(2)
    inputs(1)
    z_steps(0, 4)
    pass_on()
    middle(3)
    send_d(0)
    spread(2)
    arrive(2)
    weights(2)
    z_first(SECOND, NEAR_STEPS)
    relay_d(0)
    inputs(2)
    pass_on()
    z_steps(4, 8)
    spread(3)
    arrive(3)
    inputs(3)
    for o in (2, 1, 3):
        x_copy(o).start()
    collect_d(0, 1)
    collect_d(0, 0)
    weights(3)
    turn_q(1)
    turn_q(0)
    z_steps(8, 16)
    spread_d(0, 1)
    spread_d(0, 0)
    for o in (1, 3, 2):
        x_copy(o).wait_recv()
    mine = pl.ds(pl.multiple_of(x * XTOK, XTOK), XTOK)
    total = ig[mine, :]
    for o in range(3):
        total = total + xrecv[o].astype(F32)
    hsend[...] = total.astype(BF)
    pl.semaphore_wait(ring, 1)
    hi_copy().start()
    z_steps(16, THIRD + SKEW)
    add_d(0)
    z_steps(THIRD + SKEW, 36)
    hi_copy().wait_recv()
    agbuf[x] = (hsend[...].astype(F32) + hrecv[...].astype(F32)).astype(BF)
    for o in (2, 1, 3):
        ag_copy(o).start()
    z_steps(36, LAST)

    def finish(u, carry):
        early = u < EARLY
        from_below = dep > jnp.where(early, 0, 2)
        from_above = dep < jnp.where(early, NZ - 1, NZ - 3)
        lanes = pl.ds(pl.multiple_of(u * LANE, LANE), LANE)
        wgr_ref[:, lanes] = zterm[u, dep].astype(F32)

        @pl.when(from_below)
        def _():
            z_up(u, dep).wait_recv()
            wgr_ref[:, lanes] += zl[u, dep].astype(F32)

        @pl.when(from_above)
        def _():
            z_down(u, dep).wait_recv()
            wgr_ref[:, lanes] += zr[u, dep].astype(F32)

        return carry

    lax.fori_loop(0, UNITS, finish, 0)

    for o in (1, 3, 2):
        ag_copy(o).wait_recv()
    ig_ref[...] = agbuf[...].reshape(TOK, FEAT)

    for s in range(NS):
        core_copy(s).wait_send()
        for o in (1, 2, 3):
            y_copy(s, o).wait_send()
            gather_copy(s, o).wait_send()
        for o in range(NY):
            cross_copy(s, o).wait_send()
    for o in (1, 2, 3):
        x_copy(o).wait_send()
        ag_copy(o).wait_send()
    hi_copy().wait_send()

    @pl.when(rank < 2)
    def _():
        q_copy(rank, ownq).wait_send()
        for n in range(NM):
            d_copy(n, rank, dbuf[MOVED[n]].at[blk]).wait_send()

    @pl.when(rank == 1)
    def _():
        q_copy(0, ownq).wait_send()
        for n in range(NM):
            d_copy(n, 0, fd[n].at[0, blk]).wait_send()

    @pl.when(rank == 2)
    def _():
        for slot in range(2):
            for o in (1, 2, 3):
                fx_copy(slot, o).wait_send()
                for n in range(NM):
                    fg_copy(n, slot, o).wait_send()
            for o in range(NY):
                for n in range(NM):
                    ff_copy(n, slot, o).wait_send()

    def drain(q, carry):
        u, j = q // NZ, q % NZ
        sends = ((j > dep) & (dep >= 2)) | ((j < dep) & (dep <= NZ - 3)) | ((j != dep) & (u < EARLY))

        @pl.when(sends)
        def _():
            z_up(u, j).wait_send()

        return carry

    lax.fori_loop(0, UNITS * NZ, drain, 0)


def results(ig_ref, wgr_ref, input_ref, gate_ref, up_ref, down_ref):
    input_ref[...] = ig_ref[...].astype(F32)
    gate_ref[...] = wgr_ref[:CHUNK]
    up_ref[...] = wgr_ref[CHUNK:2 * CHUNK]
    down_ref[...] = wgr_ref[2 * CHUNK:]


def shards(layer_input, output_grad, w_gate, w_up, w_down):
    factor = float(layer_input.shape[0] * lax.axis_size("depth")) ** (-0.5)
    dma = pltpu.SemaphoreType.DMA

    def per_slice(lead, dtype):
        return [pltpu.VMEM((*lead, w), dtype) for _, w in SLICES]

    scratch = [
        pltpu.VMEM((TOK, FEAT), BF),
        pltpu.VMEM((TOK, FEAT), BF),
        pltpu.VMEM((FEAT, HID), BF),
        pltpu.VMEM((FEAT, HID), BF),
        pltpu.VMEM((HID, FEAT), BF),
        dma((5,)),
        pltpu.SemaphoreType.REGULAR,
        pltpu.VMEM((2, FEAT, TOK), BF),
        *per_slice((3, HALF), F32),
        *per_slice((3, HALF), BF),
        *per_slice((3, HALF), BF),
        *per_slice((NY, 3, QUART), BF),
        *per_slice((NY - 1, 3, QUART), BF),
        *per_slice((2 * NY, 3, QUART), BF),
        pltpu.VMEM((UNITS, NZ, ROWS, LANE), BF),
        pltpu.VMEM((UNITS, NZ, ROWS, LANE), BF),
        pltpu.VMEM((UNITS, NZ, ROWS, LANE), BF),
        pltpu.VMEM((TOK, FEAT), F32),
        pltpu.VMEM((NX, XTOK, FEAT), BF),
        pltpu.VMEM((NX - 1, XTOK, FEAT), BF),
        pltpu.VMEM((XTOK, FEAT), BF),
        pltpu.VMEM((XTOK, FEAT), BF),
        pltpu.VMEM((NX, XTOK, FEAT), BF),
        pltpu.VMEM((2, XTOK, FEAT), BF),
        pltpu.VMEM((2, NX, 2, XTOK, FEAT), BF),
        pltpu.VMEM((2, 2, FEAT, TOK), BF),
        pltpu.VMEM((LATE, NZ, ROWS, LANE), F32),
        *[pltpu.VMEM((2, 2 * NY, 3, QUART, SLICES[s][1]), BF) for s in MOVED],
        dma((NS,)), dma((NS,)),
        dma((NS, 3)), dma((NS, 3)),
        dma((NS, 3)), dma((NS, 3)),
        dma((NS, NY)), dma((NS, NY)),
        dma((UNITS, NZ)), dma((UNITS, NZ)), dma((UNITS, NZ)),
        dma((3,)), dma((3,)),
        dma((1,)), dma((1,)),
        dma((3,)), dma((3,)),
        dma((2,)), dma((2,)),
        dma((NM, 2)), dma((NM, 2)),
        dma((2, 3)), dma((2, 3)),
        dma((NM, 2, 3)), dma((NM, 2, 3)),
        dma((NM, 2, NY)), dma((NM, 2, NY)),
    ]
    vmem = pl.BlockSpec(memory_space=pltpu.VMEM)
    ig, wgr = pl.pallas_call(
        lambda *refs: kernel(factor, *refs),
        out_shape=(
            jax.ShapeDtypeStruct((TOK, FEAT), BF),
            jax.ShapeDtypeStruct((ROWS, HID), F32),
        ),
        in_specs=[pl.BlockSpec(memory_space=pl.ANY)] * 5,
        out_specs=(vmem, vmem),
        scratch_shapes=scratch,
        compiler_params=pltpu.CompilerParams(
            collective_id=0, has_side_effects=True, vmem_limit_bytes=56 * 2 ** 20
        ),
        name="swiglu_back",
    )(layer_input, output_grad, w_gate, w_up, w_down)
    input_grad, gate_grad, up_grad, down_grad = pl.pallas_call(
        results,
        out_shape=(
            jax.ShapeDtypeStruct((TOK, FEAT), F32),
            jax.ShapeDtypeStruct((CHUNK, HID), F32),
            jax.ShapeDtypeStruct((CHUNK, HID), F32),
            jax.ShapeDtypeStruct((CHUNK, HID), F32),
        ),
        in_specs=[vmem] * 2,
        out_specs=(vmem,) * 4,
        name="results",
    )(ig, wgr)
    return input_grad, gate_grad, up_grad, down_grad.T


def solution(mesh):
    in_specs = (
        P("depth", "row"),
        P("depth", "row"),
        P("row", "col"),
        P("row", "col"),
        P("col", "row"),
    )
    out_specs = (
        P("depth", "row"),
        P(("row", "depth"), "col"),
        P(("row", "depth"), "col"),
        P("col", ("row", "depth")),
    )
    return jax.shard_map(shards, mesh=mesh, in_specs=in_specs, out_specs=out_specs, check_vma=False)
```

```python
import jax
import jax.numpy as jnp
from jax import lax
from jax.experimental import pallas as pl
from jax.experimental.pallas import tpu as pltpu
from jax.sharding import PartitionSpec as P

MESH = pl.DeviceIdType.MESH
BF, F32 = jnp.bfloat16, jnp.float32

NY, NX, NZ = 4, 4, 8
TOK, FEAT, HID = 512, 640, 896
HALF = TOK // 2
QUART = HALF // NY
XTOK = TOK // NX
CHUNK = FEAT // NZ
ROWS = 3 * CHUNK
LANE = 128
UNITS = HID // LANE
SLICES = ((0, 128), (128, 128), (256, 256), (512, 384))
NS = len(SLICES)
HOPS = NZ - 1
EARLY = 4
LATE = UNITS - EARLY
MOVED = (3,)
NM = len(MOVED)
SKEW = 4
PIECES = 4
PTOK = XTOK // PIECES
FAR = HOPS - 2
FIRST = HOPS
SECOND = FIRST + FAR
THIRD = SECOND + (EARLY - 2) * FAR
NEAR_STEPS = EARLY * HOPS
FAR_STEPS = THIRD + LATE * FAR
LAST = THIRD + max(LATE * (HOPS - d) + SKEW * (d - 1) for d in range(2, HOPS))


def swiglu_back(gate, up, back):
    sig = jax.nn.sigmoid(gate)
    silu = gate * sig
    d_gate = (back * up * sig * (1.0 + gate * (1.0 - sig))).astype(BF)
    return d_gate, (back * silu).astype(BF), (silu * up).astype(BF)


def dot(a, b):
    return jnp.dot(a, b, preferred_element_type=F32)


def dot_last(a, b):
    return lax.dot_general(a, b, (((1,), (1,)), ((), ())), preferred_element_type=F32)


def kernel(factor, x_in, g_in, wg_in, wu_in, wd_in, ig_ref, wgr_ref, *scratch):
    it = iter(scratch)
    x_ref, g_ref, wg_ref, wu_ref, wd_ref, loads, ring = (next(it) for _ in range(7))
    load = [
        pltpu.make_async_copy(src, dst, loads.at[n])
        for n, (src, dst) in enumerate(
            ((x_in, x_ref), (wg_in, wg_ref), (wu_in, wu_ref), (g_in, g_ref), (wd_in, wd_ref))
        )
    ]
    for c in load:
        c.start()
    xt = next(it)
    ph = [next(it) for _ in SLICES]
    csend = [next(it) for _ in SLICES]
    crecv = [next(it) for _ in SLICES]
    ysend = [next(it) for _ in SLICES]
    yrecv = [next(it) for _ in SLICES]
    dbuf = [next(it) for _ in SLICES]
    zterm, zl, zr = next(it), next(it), next(it)
    ig, xsend, xrecv, hsend, hrecv, agbuf = (next(it) for _ in range(6))
    ownq, fq, xt2, fsum = next(it), next(it), next(it), next(it)
    fd = [next(it) for _ in MOVED]
    cs, cr, ys, yr, gs, gr, fs, fr, zs, zlr, zrr, xs, xr, hs, hr, ags, agr, *it = it
    qs, qr, ds, dr, fxs, fxr, fgs, fgr, ffs, ffr = it

    row, col, dep = lax.axis_index("row"), lax.axis_index("col"), lax.axis_index("depth")
    y, k = row // 2, row % 2
    x, zh = col // 2, col % 2
    other = (y * 2 + 1 - k, col, dep)

    def at_y(o):
        return (((y + o) % NY) * 2 + k, col, dep)

    def at_x(o):
        return (row, ((x + o) % NX) * 2 + zh, dep)

    partner = (row, x * 2 + 1 - zh, dep)
    up_z = (row, x * 2 + (zh + (dep + 1) // NZ) % 2, (dep + 1) % NZ)
    down_z = (row, x * 2 + (zh + 1 - (dep + NZ - 1) // NZ) % 2, (dep + NZ - 1) % NZ)

    barrier = pltpu.get_barrier_semaphore()
    near = [at_y(1), at_y(2), at_y(3), at_x(1), at_x(2), at_x(3), other, up_z, down_z]
    for dev in near:
        pl.semaphore_signal(barrier, inc=1, device_id=dev, device_id_type=MESH)

    left = dep < NZ // 2
    rank = jnp.where(left, dep, NZ - 1 - dep)
    inward = (row, col, jnp.where(left, dep + 1, dep - 1))
    blk = k * NY + y

    def tell():
        pl.semaphore_signal(ring, inc=1, device_id=up_z, device_id_type=MESH)

    def pass_on():
        pl.semaphore_wait(ring, 1)
        tell()

    def copy(src, dst, ssem, rsem, dev):
        return pltpu.make_async_remote_copy(
            src_ref=src, dst_ref=dst, send_sem=ssem, recv_sem=rsem, device_id=dev, device_id_type=MESH
        )

    def partials(half, s, loaded):
        lo, w = SLICES[s]
        rows = pl.ds(pl.multiple_of(half * HALF, HALF), HALF)
        if not loaded:
            load[0].wait()
            load[1].wait()
        yield dot(x_ref[rows, :], wg_ref[:, lo:lo + w])
        if not loaded:
            load[2].wait()
        yield dot(x_ref[rows, :], wu_ref[:, lo:lo + w])
        if not loaded:
            load[3].wait()
            load[4].wait()
        yield dot_last(g_ref[rows, :], wd_ref[lo:lo + w, :])

    def core_copy(s):
        return copy(csend[s], crecv[s], cs.at[s], cr.at[s], other)

    def first(s):
        for m, part in enumerate(partials(1 - k, s, s > 0)):
            csend[s][m] = part.astype(BF)
        if s == 0:
            pl.semaphore_wait(barrier, len(near))
            tell()
        core_copy(s).start()
        for m, part in enumerate(partials(k, s, True)):
            ph[s][m] = part

    def y_copy(s, o):
        return copy(ysend[s].at[(y + o) % NY], yrecv[s].at[o - 1], ys.at[s, o - 1], yr.at[s, o - 1], at_y(o))

    def reduce_core(s):
        core_copy(s).wait_recv()
        for m in range(3):
            total = ph[s][m] + crecv[s][m].astype(F32)
            ph[s][m] = total
            for b in range(NY):
                ysend[s][b, m] = total[b * QUART:(b + 1) * QUART].astype(BF)
        for o in (2, 1, 3):
            y_copy(s, o).start()

    def gather_copy(s, o):
        return copy(dbuf[s].at[blk], dbuf[s].at[blk], gs.at[s, o - 1], gr.at[s, o - 1], at_y(o))

    def cross_copy(s, o):
        b = k * NY + (y - o + NY) % NY
        return copy(dbuf[s].at[b], dbuf[s].at[b], fs.at[s, o], fr.at[s, o], other)

    def middle(s):
        for o in (1, 2, 3):
            y_copy(s, o).wait_recv()
        own = pl.ds(pl.multiple_of(y * QUART, QUART), QUART)
        sums = []
        for m in range(3):
            total = ph[s][m, own, :]
            for o in range(3):
                total = total + yrecv[s][o, m].astype(F32)
            sums.append(total)
        for m, value in enumerate(swiglu_back(*sums)):
            dbuf[s][blk, m] = value
        for o in (2, 1, 3):
            gather_copy(s, o).start()
        cross_copy(s, 0).start()

    def spread(s):
        for o in (1, 3, 2):
            gather_copy(s, o).wait_recv()
            cross_copy(s, o).start()

    def arrive(s):
        for o in range(NY):
            cross_copy(s, o).wait_recv()

    def hidden(s, m):
        return dbuf[s][:, m].reshape(TOK, SLICES[s][1])

    def inputs(s):
        lo, w = SLICES[s]
        part = dot_last(hidden(s, 0), wg_ref[:, lo:lo + w]) + dot_last(hidden(s, 1), wu_ref[:, lo:lo + w])
        if s == 0:
            ig[...] = part
        elif s < NS - 1:
            ig[...] += part
        else:
            total = ig[...] + part
            ig[...] = total
            for b in range(NX):
                xsend[b] = total[b * XTOK:(b + 1) * XTOK].astype(BF)

    def weights(s):
        lo, w = SLICES[s]
        for m in range(3):
            term = (dot(xt[m // 2], hidden(s, m)) * factor).astype(BF)
            for v in range(w // LANE):
                for j in range(NZ):
                    zterm[lo // LANE + v, j, m * CHUNK:(m + 1) * CHUNK, :] = term[
                        j * CHUNK:(j + 1) * CHUNK, v * LANE:(v + 1) * LANE
                    ]

    def z_up(u, j):
        return copy(zterm.at[u, j], zl.at[u, j], zs.at[u, j], zlr.at[u, j], up_z)

    def z_down(u, j):
        return copy(zterm.at[u, j], zr.at[u, j], zs.at[u, j], zrr.at[u, j], down_z)

    def z_first(lo, hi):
        def send(q, carry):
            _, u, n = place(q, False)

            @pl.when(dep == 0)
            def _():
                z_up(u, HOPS - n).start()

            @pl.when(dep == NZ - 1)
            def _():
                z_down(u, n).start()

            return carry

        lax.fori_loop(lo, hi, send, 0)

    def forward_up(u, j, waits):
        @pl.when(waits)
        def _():
            z_up(u, j).wait_recv()
            zterm[u, j] = (zterm[u, j].astype(F32) + zl[u, j].astype(F32)).astype(BF)

        z_up(u, j).start()

    def forward_down(u, j, waits):
        @pl.when(waits)
        def _():
            z_down(u, j).wait_recv()
            zterm[u, j] = (zterm[u, j].astype(F32) + zr[u, j].astype(F32)).astype(BF)

        z_down(u, j).start()

    def place(q, far):
        late = far & (q >= THIRD)
        r2, r3 = jnp.maximum(q - SECOND, 0), jnp.maximum(q - THIRD, 0)
        u = jnp.where(late, EARLY + r3 % LATE, 1 + r3 % (EARLY - 1))
        u = jnp.where(q < THIRD, 2 + r2 % (EARLY - 2), u)
        u = jnp.where(q < SECOND, jnp.where(q < FIRST, 0, 1), u)
        n = jnp.where(late, r3 // LATE, FAR + r3 // (EARLY - 1))
        n = jnp.where(q < THIRD, r2 // (EARLY - 2), n)
        n = jnp.where(q < SECOND, jnp.where(q < FIRST, q, q - FIRST), n)
        return late, u, n

    def z_step(t, carry):
        q = t - SKEW * (dep - 1)
        end = jnp.where(dep >= 2, FAR_STEPS, NEAR_STEPS)
        late, u, j = place(jnp.clip(q, 0, end - 1), dep >= 2)
        j = HOPS - j

        @pl.when((q >= 0) & (q < end) & (j > dep) & (dep > 0))
        def _():
            forward_up(u, j, dep > jnp.where(late, 2, 0))

        p = t - SKEW * (NZ - 2 - dep)
        end = jnp.where(dep <= NZ - 3, FAR_STEPS, NEAR_STEPS)
        late, v, i = place(jnp.clip(p, 0, end - 1), dep <= NZ - 3)

        @pl.when((p >= 0) & (p < end) & (i < dep) & (dep < NZ - 1))
        def _():
            forward_down(v, i, dep < jnp.where(late, NZ - 3, NZ - 1))

        return carry

    def z_steps(lo, hi):
        lax.fori_loop(lo, hi, z_step, 0)

    def q_copy(slot, src):
        return copy(src, fq.at[slot, x], qs.at[slot], qr.at[slot], inward)

    def d_copy(n, slot, src):
        return copy(src, fd[n].at[slot, blk], ds.at[n, slot], dr.at[n, slot], inward)

    def fx_copy(slot, o):
        return copy(fq.at[slot, x], fq.at[slot, x], fxs.at[slot, o - 1], fxr.at[slot, o - 1], at_x(o))

    def fg_copy(n, slot, o):
        return copy(
            fd[n].at[slot, blk], fd[n].at[slot, blk], fgs.at[n, slot, o - 1], fgr.at[n, slot, o - 1], at_y(o)
        )

    def ff_copy(n, slot, o):
        b = k * NY + (y - o + NY) % NY
        return copy(fd[n].at[slot, b], fd[n].at[slot, b], ffs.at[n, slot, o], ffr.at[n, slot, o], other)

    def send_q():
        @pl.when(rank < 2)
        def _():
            part = pl.ds(pl.multiple_of(x * XTOK, XTOK), XTOK)
            ownq[0] = x_ref[part, :]
            ownq[1] = g_ref[part, :]
            q_copy(rank, ownq).start()

    def relay_q():
        @pl.when(rank == 1)
        def _():
            q_copy(0, fq.at[0, x]).wait_recv()
            q_copy(0, fq.at[0, x]).start()

    def collect_q(slot):
        @pl.when(rank == 2)
        def _():
            q_copy(slot, ownq).wait_recv()
            for o in (2, 1, 3):
                fx_copy(slot, o).start()

    def turn_q(slot):
        @pl.when(rank == 2)
        def _():
            for o in (1, 3, 2):
                fx_copy(slot, o).wait_recv()
            for m in range(2):
                xt2[slot, m] = fq[slot, :, m].reshape(TOK, FEAT).T

    def send_d(n):
        @pl.when(rank < 2)
        def _():
            d_copy(n, rank, dbuf[MOVED[n]].at[blk]).start()

    def relay_d(n):
        @pl.when(rank == 1)
        def _():
            d_copy(n, 0, fd[n].at[0, blk]).wait_recv()
            d_copy(n, 0, fd[n].at[0, blk]).start()

    def collect_d(n, slot):
        @pl.when(rank == 2)
        def _():
            d_copy(n, slot, fd[n].at[slot, blk]).wait_recv()
            for o in (2, 1, 3):
                fg_copy(n, slot, o).start()
            ff_copy(n, slot, 0).start()

    def spread_d(n, slot):
        @pl.when(rank == 2)
        def _():
            for o in (1, 3, 2):
                fg_copy(n, slot, o).wait_recv()
                ff_copy(n, slot, o).start()

    def add_d(n):
        @pl.when(rank == 2)
        def _():
            lo, w = SLICES[MOVED[n]]
            for slot in range(2):
                for o in range(NY):
                    ff_copy(n, slot, o).wait_recv()
                for m in range(3):
                    term = dot(xt2[slot, m // 2], fd[n][slot, :, m].reshape(TOK, w)) * factor
                    for j in range(NZ):
                        counts = jnp.where(left, j, NZ - 1 - j) > slot
                        for v in range(w // LANE):
                            u = lo // LANE + v
                            rows = slice(m * CHUNK, (m + 1) * CHUNK)
                            more = term[j * CHUNK:(j + 1) * CHUNK, v * LANE:(v + 1) * LANE]
                            fsum[u - EARLY, j, rows, :] = (
                                fsum[u - EARLY, j, rows, :] + jnp.where(counts, more, 0.0)
                                if slot else jnp.where(counts, more, 0.0)
                            )
                            if slot:
                                zterm[u, j, rows, :] = (
                                    zterm[u, j, rows, :].astype(F32) + fsum[u - EARLY, j, rows, :]
                                ).astype(BF)

    def x_copy(o):
        return copy(xsend.at[(x + o) % NX], xrecv.at[o - 1], xs.at[o - 1], xr.at[o - 1], at_x(o))

    def hi_copy(n):
        return copy(hsend.at[n], hrecv.at[n], hs.at[n], hr.at[n], partner)

    def ag_copy(n, o):
        return copy(agbuf.at[x, n], agbuf.at[x, n], ags.at[n, o - 1], agr.at[n, o - 1], at_x(o))

    def sum_x():
        for o in (1, 3, 2):
            x_copy(o).wait_recv()
        mine = pl.ds(pl.multiple_of(x * XTOK, XTOK), XTOK)
        total = ig[mine, :]
        for o in range(3):
            total = total + xrecv[o].astype(F32)
        for n in range(PIECES):
            hsend[n] = total[n * PTOK:(n + 1) * PTOK].astype(BF)
        pl.semaphore_wait(ring, 1)

    def gather_x(n):
        hi_copy(n).wait_recv()
        agbuf[x, n] = (hsend[n].astype(F32) + hrecv[n].astype(F32)).astype(BF)
        for o in (2, 1, 3):
            ag_copy(n, o).start()

    first(0)
    send_q()
    first(1)
    reduce_core(0)
    xt[0] = x_ref[...].T
    xt[1] = g_ref[...].T
    pass_on()
    first(2)
    middle(0)
    reduce_core(1)
    pass_on()
    first(3)
    reduce_core(2)
    relay_q()
    spread(0)
    arrive(0)
    weights(0)
    z_first(0, FIRST)
    collect_q(1)
    pass_on()
    middle(1)
    reduce_core(3)
    inputs(0)
    pass_on()
    spread(1)
    arrive(1)
    weights(1)
    z_first(FIRST, SECOND)
    collect_q(0)
    pass_on()
    middle(2)
    inputs(1)
    z_steps(0, 4)
    pass_on()
    middle(3)
    send_d(0)
    spread(2)
    arrive(2)
    weights(2)
    z_first(SECOND, NEAR_STEPS)
    relay_d(0)
    inputs(2)
    pass_on()
    z_steps(4, 8)
    collect_d(0, 1)
    spread(3)
    arrive(3)
    collect_d(0, 0)
    inputs(3)
    for o in (2, 1, 3):
        x_copy(o).start()
    weights(3)
    turn_q(1)
    turn_q(0)
    z_steps(8, 14)
    sum_x()
    hi_copy(0).start()
    z_steps(14, 17)
    hi_copy(1).start()
    spread_d(0, 1)
    spread_d(0, 0)
    z_steps(17, 21)
    hi_copy(2).start()
    z_steps(21, THIRD + SKEW)
    hi_copy(3).start()
    add_d(0)
    z_steps(THIRD + SKEW, 30)
    gather_x(0)
    z_steps(30, 33)
    gather_x(1)
    z_steps(33, 36)
    gather_x(2)
    z_steps(36, 39)
    gather_x(3)
    z_steps(39, 41)

    def finish(u, carry):
        early = u < EARLY
        from_below = dep > jnp.where(early, 0, 2)
        from_above = dep < jnp.where(early, NZ - 1, NZ - 3)
        lanes = pl.ds(pl.multiple_of(u * LANE, LANE), LANE)
        wgr_ref[:, lanes] = zterm[u, dep].astype(F32)

        @pl.when(from_below)
        def _():
            z_up(u, dep).wait_recv()
            wgr_ref[:, lanes] += zl[u, dep].astype(F32)

        @pl.when(from_above)
        def _():
            z_down(u, dep).wait_recv()
            wgr_ref[:, lanes] += zr[u, dep].astype(F32)

        return carry

    lax.fori_loop(0, EARLY, finish, 0)

    for s in range(NS):
        core_copy(s).wait_send()
        for o in (1, 2, 3):
            y_copy(s, o).wait_send()
            gather_copy(s, o).wait_send()
        for o in range(NY):
            cross_copy(s, o).wait_send()
    for o in (1, 2, 3):
        x_copy(o).wait_send()
    for n in range(PIECES):
        hi_copy(n).wait_send()

    @pl.when(rank < 2)
    def _():
        q_copy(rank, ownq).wait_send()
        for n in range(NM):
            d_copy(n, rank, dbuf[MOVED[n]].at[blk]).wait_send()

    @pl.when(rank == 1)
    def _():
        q_copy(0, ownq).wait_send()
        for n in range(NM):
            d_copy(n, 0, fd[n].at[0, blk]).wait_send()

    @pl.when(rank == 2)
    def _():
        for slot in range(2):
            for o in (1, 2, 3):
                fx_copy(slot, o).wait_send()
                for n in range(NM):
                    fg_copy(n, slot, o).wait_send()
            for o in range(NY):
                for n in range(NM):
                    ff_copy(n, slot, o).wait_send()

    z_steps(41, LAST)
    for n in range(PIECES):
        for o in (1, 3, 2):
            ag_copy(n, o).wait_recv()
    out = pltpu.make_async_copy(agbuf, ig_ref, loads.at[0])
    out.start()
    lax.fori_loop(EARLY, UNITS, finish, 0)
    for n in range(PIECES):
        for o in (1, 2, 3):
            ag_copy(n, o).wait_send()

    def drain(q, carry):
        u, j = q // NZ, q % NZ
        sends = ((j > dep) & (dep >= 2)) | ((j < dep) & (dep <= NZ - 3)) | ((j != dep) & (u < EARLY))

        @pl.when(sends)
        def _():
            z_up(u, j).wait_send()

        return carry

    lax.fori_loop(0, UNITS * NZ, drain, 0)
    out.wait()


def results(ig_ref, wgr_ref, input_ref, gate_ref, up_ref, down_ref):
    input_ref[...] = ig_ref[...].astype(F32)
    gate_ref[...] = wgr_ref[:CHUNK]
    up_ref[...] = wgr_ref[CHUNK:2 * CHUNK]
    down_ref[...] = wgr_ref[2 * CHUNK:]


def shards(layer_input, output_grad, w_gate, w_up, w_down):
    factor = float(layer_input.shape[0] * lax.axis_size("depth")) ** (-0.5)
    dma = pltpu.SemaphoreType.DMA

    def per_slice(lead, dtype):
        return [pltpu.VMEM((*lead, w), dtype) for _, w in SLICES]

    scratch = [
        pltpu.VMEM((TOK, FEAT), BF),
        pltpu.VMEM((TOK, FEAT), BF),
        pltpu.VMEM((FEAT, HID), BF),
        pltpu.VMEM((FEAT, HID), BF),
        pltpu.VMEM((HID, FEAT), BF),
        dma((5,)),
        pltpu.SemaphoreType.REGULAR,
        pltpu.VMEM((2, FEAT, TOK), BF),
        *per_slice((3, HALF), F32),
        *per_slice((3, HALF), BF),
        *per_slice((3, HALF), BF),
        *per_slice((NY, 3, QUART), BF),
        *per_slice((NY - 1, 3, QUART), BF),
        *per_slice((2 * NY, 3, QUART), BF),
        pltpu.VMEM((UNITS, NZ, ROWS, LANE), BF),
        pltpu.VMEM((UNITS, NZ, ROWS, LANE), BF),
        pltpu.VMEM((UNITS, NZ, ROWS, LANE), BF),
        pltpu.VMEM((TOK, FEAT), F32),
        pltpu.VMEM((NX, XTOK, FEAT), BF),
        pltpu.VMEM((NX - 1, XTOK, FEAT), BF),
        pltpu.VMEM((PIECES, PTOK, FEAT), BF),
        pltpu.VMEM((PIECES, PTOK, FEAT), BF),
        pltpu.VMEM((NX, PIECES, PTOK, FEAT), BF),
        pltpu.VMEM((2, XTOK, FEAT), BF),
        pltpu.VMEM((2, NX, 2, XTOK, FEAT), BF),
        pltpu.VMEM((2, 2, FEAT, TOK), BF),
        pltpu.VMEM((LATE, NZ, ROWS, LANE), F32),
        *[pltpu.VMEM((2, 2 * NY, 3, QUART, SLICES[s][1]), BF) for s in MOVED],
        dma((NS,)), dma((NS,)),
        dma((NS, 3)), dma((NS, 3)),
        dma((NS, 3)), dma((NS, 3)),
        dma((NS, NY)), dma((NS, NY)),
        dma((UNITS, NZ)), dma((UNITS, NZ)), dma((UNITS, NZ)),
        dma((3,)), dma((3,)),
        dma((PIECES,)), dma((PIECES,)),
        dma((PIECES, 3)), dma((PIECES, 3)),
        dma((2,)), dma((2,)),
        dma((NM, 2)), dma((NM, 2)),
        dma((2, 3)), dma((2, 3)),
        dma((NM, 2, 3)), dma((NM, 2, 3)),
        dma((NM, 2, NY)), dma((NM, 2, NY)),
    ]
    vmem = pl.BlockSpec(memory_space=pltpu.VMEM)
    ig, wgr = pl.pallas_call(
        lambda *refs: kernel(factor, *refs),
        out_shape=(
            jax.ShapeDtypeStruct((NX, PIECES, PTOK, FEAT), BF),
            jax.ShapeDtypeStruct((ROWS, HID), F32),
        ),
        in_specs=[pl.BlockSpec(memory_space=pl.ANY)] * 5,
        out_specs=(pl.BlockSpec(memory_space=pl.ANY), vmem),
        scratch_shapes=scratch,
        compiler_params=pltpu.CompilerParams(
            collective_id=0, has_side_effects=True, vmem_limit_bytes=56 * 2 ** 20
        ),
        name="swiglu_back",
    )(layer_input, output_grad, w_gate, w_up, w_down)
    input_grad, gate_grad, up_grad, down_grad = pl.pallas_call(
        results,
        out_shape=(
            jax.ShapeDtypeStruct((TOK, FEAT), F32),
            jax.ShapeDtypeStruct((CHUNK, HID), F32),
            jax.ShapeDtypeStruct((CHUNK, HID), F32),
            jax.ShapeDtypeStruct((CHUNK, HID), F32),
        ),
        in_specs=[vmem] * 2,
        out_specs=(vmem,) * 4,
        name="results",
    )(ig.reshape(TOK, FEAT), wgr)
    return input_grad, gate_grad, up_grad, down_grad.T


def solution(mesh):
    in_specs = (
        P("depth", "row"),
        P("depth", "row"),
        P("row", "col"),
        P("row", "col"),
        P("col", "row"),
    )
    out_specs = (
        P("depth", "row"),
        P(("row", "depth"), "col"),
        P(("row", "depth"), "col"),
        P("col", ("row", "depth")),
    )
    return jax.shard_map(shards, mesh=mesh, in_specs=in_specs, out_specs=out_specs, check_vma=False)
```

```python
import jax
import jax.numpy as jnp
from jax import lax
from jax.experimental import pallas as pl
from jax.experimental.pallas import tpu as pltpu
from jax.sharding import PartitionSpec as P

MESH = pl.DeviceIdType.MESH
BF, F32 = jnp.bfloat16, jnp.float32

NY, NX, NZ = 4, 4, 8
TOK, FEAT, HID = 512, 640, 896
HALF = TOK // 2
QUART = HALF // NY
XTOK = TOK // NX
CHUNK = FEAT // NZ
ROWS = 3 * CHUNK
LANE = 128
UNITS = HID // LANE
SLICES = ((0, 128), (128, 128), (256, 256), (512, 384))
NS = len(SLICES)
HOPS = NZ - 1
EARLY = 4
LATE = UNITS - EARLY
MOVED = (3,)
NM = len(MOVED)
SKEW = 4
PIECES = 4
PTOK = XTOK // PIECES
FAR = HOPS - 2
FIRST = HOPS
SECOND = FIRST + FAR
THIRD = SECOND + (EARLY - 2) * FAR
NEAR_STEPS = EARLY * HOPS
FAR_STEPS = THIRD + LATE * FAR
LAST = THIRD + max(LATE * (HOPS - d) + SKEW * (d - 1) for d in range(2, HOPS))


def swiglu_back(gate, up, back):
    sig = jax.nn.sigmoid(gate)
    silu = gate * sig
    d_gate = (back * up * sig * (1.0 + gate * (1.0 - sig))).astype(BF)
    return d_gate, (back * silu).astype(BF), (silu * up).astype(BF)


def dot(a, b):
    return jnp.dot(a, b, preferred_element_type=F32)


def dot_last(a, b):
    return lax.dot_general(a, b, (((1,), (1,)), ((), ())), preferred_element_type=F32)


def kernel(factor, x_in, g_in, wg_in, wu_in, wd_in, ig_ref, wgr_ref, *scratch):
    it = iter(scratch)
    x_ref, g_ref, wg_ref, wu_ref, wd_ref, loads, ring = (next(it) for _ in range(7))
    load = [
        pltpu.make_async_copy(src, dst, loads.at[n])
        for n, (src, dst) in enumerate(
            ((x_in, x_ref), (wg_in, wg_ref), (wu_in, wu_ref), (g_in, g_ref), (wd_in, wd_ref))
        )
    ]
    for c in load:
        c.start()
    xt = next(it)
    ph = [next(it) for _ in SLICES]
    csend = [next(it) for _ in SLICES]
    crecv = [next(it) for _ in SLICES]
    ysend = [next(it) for _ in SLICES]
    yrecv = [next(it) for _ in SLICES]
    dbuf = [next(it) for _ in SLICES]
    zterm, zl, zr = next(it), next(it), next(it)
    ig, xsend, xrecv, hsend, hrecv, agbuf = (next(it) for _ in range(6))
    ownq, fq, xt2, fsum = next(it), next(it), next(it), next(it)
    fd = [next(it) for _ in MOVED]
    cs, cr, ys, yr, gs, gr, fs, fr, zs, zlr, zrr, xs, xr, hs, hr, ags, agr, *it = it
    qs, qr, ds, dr, fxs, fxr, fgs, fgr, ffs, ffr = it

    row, col, dep = lax.axis_index("row"), lax.axis_index("col"), lax.axis_index("depth")
    y, k = row // 2, row % 2
    x, zh = col // 2, col % 2
    other = (y * 2 + 1 - k, col, dep)

    def at_y(o):
        return (((y + o) % NY) * 2 + k, col, dep)

    def at_x(o):
        return (row, ((x + o) % NX) * 2 + zh, dep)

    partner = (row, x * 2 + 1 - zh, dep)
    up_z = (row, x * 2 + (zh + (dep + 1) // NZ) % 2, (dep + 1) % NZ)
    down_z = (row, x * 2 + (zh + 1 - (dep + NZ - 1) // NZ) % 2, (dep + NZ - 1) % NZ)

    barrier = pltpu.get_barrier_semaphore()
    near = [at_y(1), at_y(2), at_y(3), at_x(1), at_x(2), at_x(3), other, up_z, down_z]
    for dev in near:
        pl.semaphore_signal(barrier, inc=1, device_id=dev, device_id_type=MESH)

    left = dep < NZ // 2
    rank = jnp.where(left, dep, NZ - 1 - dep)
    inward = (row, col, jnp.where(left, dep + 1, dep - 1))
    blk = k * NY + y

    def tell():
        pl.semaphore_signal(ring, inc=1, device_id=up_z, device_id_type=MESH)

    def pass_on():
        pl.semaphore_wait(ring, 1)
        tell()

    def copy(src, dst, ssem, rsem, dev):
        return pltpu.make_async_remote_copy(
            src_ref=src, dst_ref=dst, send_sem=ssem, recv_sem=rsem, device_id=dev, device_id_type=MESH
        )

    def partials(half, s, loaded):
        lo, w = SLICES[s]
        rows = pl.ds(pl.multiple_of(half * HALF, HALF), HALF)
        if not loaded:
            load[0].wait()
            load[1].wait()
        yield dot(x_ref[rows, :], wg_ref[:, lo:lo + w])
        if not loaded:
            load[2].wait()
        yield dot(x_ref[rows, :], wu_ref[:, lo:lo + w])
        if not loaded:
            load[3].wait()
            load[4].wait()
        yield dot_last(g_ref[rows, :], wd_ref[lo:lo + w, :])

    def core_copy(s):
        return copy(csend[s], crecv[s], cs.at[s], cr.at[s], other)

    def first(s):
        for m, part in enumerate(partials(1 - k, s, s > 0)):
            csend[s][m] = part.astype(BF)
        if s == 0:
            pl.semaphore_wait(barrier, len(near))
            tell()
        core_copy(s).start()
        for m, part in enumerate(partials(k, s, True)):
            ph[s][m] = part

    def y_copy(s, o):
        return copy(ysend[s].at[(y + o) % NY], yrecv[s].at[o - 1], ys.at[s, o - 1], yr.at[s, o - 1], at_y(o))

    def reduce_core(s):
        core_copy(s).wait_recv()
        for m in range(3):
            total = ph[s][m] + crecv[s][m].astype(F32)
            ph[s][m] = total
            for b in range(NY):
                ysend[s][b, m] = total[b * QUART:(b + 1) * QUART].astype(BF)
        for o in (2, 1, 3):
            y_copy(s, o).start()

    def gather_copy(s, o):
        return copy(dbuf[s].at[blk], dbuf[s].at[blk], gs.at[s, o - 1], gr.at[s, o - 1], at_y(o))

    def cross_copy(s, o):
        b = k * NY + (y - o + NY) % NY
        return copy(dbuf[s].at[b], dbuf[s].at[b], fs.at[s, o], fr.at[s, o], other)

    def middle(s):
        for o in (1, 2, 3):
            y_copy(s, o).wait_recv()
        own = pl.ds(pl.multiple_of(y * QUART, QUART), QUART)
        sums = []
        for m in range(3):
            total = ph[s][m, own, :]
            for o in range(3):
                total = total + yrecv[s][o, m].astype(F32)
            sums.append(total)
        for m, value in enumerate(swiglu_back(*sums)):
            dbuf[s][blk, m] = value
        for o in (2, 1, 3):
            gather_copy(s, o).start()
        cross_copy(s, 0).start()

    def spread(s):
        for o in (1, 3, 2):
            gather_copy(s, o).wait_recv()
            cross_copy(s, o).start()

    def arrive(s):
        for o in range(NY):
            cross_copy(s, o).wait_recv()

    def hidden(s, m):
        return dbuf[s][:, m].reshape(TOK, SLICES[s][1])

    def inputs(s):
        lo, w = SLICES[s]
        part = dot_last(hidden(s, 0), wg_ref[:, lo:lo + w]) + dot_last(hidden(s, 1), wu_ref[:, lo:lo + w])
        if s == 0:
            ig[...] = part
        elif s < NS - 1:
            ig[...] += part
        else:
            total = ig[...] + part
            ig[...] = total
            for b in range(NX):
                xsend[b] = total[b * XTOK:(b + 1) * XTOK].astype(BF)

    def weights(s):
        lo, w = SLICES[s]
        for m in range(3):
            term = (dot(xt[m // 2], hidden(s, m)) * factor).astype(BF)
            for v in range(w // LANE):
                for j in range(NZ):
                    zterm[lo // LANE + v, j, m * CHUNK:(m + 1) * CHUNK, :] = term[
                        j * CHUNK:(j + 1) * CHUNK, v * LANE:(v + 1) * LANE
                    ]

    def z_up(u, j):
        return copy(zterm.at[u, j], zl.at[u, j], zs.at[u, j], zlr.at[u, j], up_z)

    def z_down(u, j):
        return copy(zterm.at[u, j], zr.at[u, j], zs.at[u, j], zrr.at[u, j], down_z)

    def z_first(lo, hi):
        def send(q, carry):
            _, u, n = place(q, False)

            @pl.when(dep == 0)
            def _():
                z_up(u, HOPS - n).start()

            @pl.when(dep == NZ - 1)
            def _():
                z_down(u, n).start()

            return carry

        lax.fori_loop(lo, hi, send, 0)

    def forward_up(u, j, waits):
        @pl.when(waits)
        def _():
            z_up(u, j).wait_recv()
            zterm[u, j] = (zterm[u, j].astype(F32) + zl[u, j].astype(F32)).astype(BF)

        z_up(u, j).start()

    def forward_down(u, j, waits):
        @pl.when(waits)
        def _():
            z_down(u, j).wait_recv()
            zterm[u, j] = (zterm[u, j].astype(F32) + zr[u, j].astype(F32)).astype(BF)

        z_down(u, j).start()

    def place(q, far):
        late = far & (q >= THIRD)
        r2, r3 = jnp.maximum(q - SECOND, 0), jnp.maximum(q - THIRD, 0)
        u = jnp.where(late, EARLY + r3 % LATE, 1 + r3 % (EARLY - 1))
        u = jnp.where(q < THIRD, 2 + r2 % (EARLY - 2), u)
        u = jnp.where(q < SECOND, jnp.where(q < FIRST, 0, 1), u)
        n = jnp.where(late, r3 // LATE, FAR + r3 // (EARLY - 1))
        n = jnp.where(q < THIRD, r2 // (EARLY - 2), n)
        n = jnp.where(q < SECOND, jnp.where(q < FIRST, q, q - FIRST), n)
        return late, u, n

    def z_step(t, carry):
        q = t - SKEW * (dep - 1)
        end = jnp.where(dep >= 2, FAR_STEPS, NEAR_STEPS)
        late, u, j = place(jnp.clip(q, 0, end - 1), dep >= 2)
        j = HOPS - j

        @pl.when((q >= 0) & (q < end) & (j > dep) & (dep > 0))
        def _():
            forward_up(u, j, dep > jnp.where(late, 2, 0))

        p = t - SKEW * (NZ - 2 - dep)
        end = jnp.where(dep <= NZ - 3, FAR_STEPS, NEAR_STEPS)
        late, v, i = place(jnp.clip(p, 0, end - 1), dep <= NZ - 3)

        @pl.when((p >= 0) & (p < end) & (i < dep) & (dep < NZ - 1))
        def _():
            forward_down(v, i, dep < jnp.where(late, NZ - 3, NZ - 1))

        return carry

    def z_steps(lo, hi):
        lax.fori_loop(lo, hi, z_step, 0)

    def q_copy(slot, src):
        return copy(src, fq.at[slot, x], qs.at[slot], qr.at[slot], inward)

    def d_copy(n, slot, src):
        return copy(src, fd[n].at[slot, blk], ds.at[n, slot], dr.at[n, slot], inward)

    def fx_copy(slot, o):
        return copy(fq.at[slot, x], fq.at[slot, x], fxs.at[slot, o - 1], fxr.at[slot, o - 1], at_x(o))

    def fg_copy(n, slot, o):
        return copy(
            fd[n].at[slot, blk], fd[n].at[slot, blk], fgs.at[n, slot, o - 1], fgr.at[n, slot, o - 1], at_y(o)
        )

    def ff_copy(n, slot, o):
        b = k * NY + (y - o + NY) % NY
        return copy(fd[n].at[slot, b], fd[n].at[slot, b], ffs.at[n, slot, o], ffr.at[n, slot, o], other)

    def send_q():
        @pl.when(rank < 2)
        def _():
            part = pl.ds(pl.multiple_of(x * XTOK, XTOK), XTOK)
            ownq[0] = x_ref[part, :]
            ownq[1] = g_ref[part, :]
            q_copy(rank, ownq).start()

    def relay_q():
        @pl.when(rank == 1)
        def _():
            q_copy(0, fq.at[0, x]).wait_recv()
            q_copy(0, fq.at[0, x]).start()

    def collect_q(slot):
        @pl.when(rank == 2)
        def _():
            q_copy(slot, ownq).wait_recv()
            for o in (2, 1, 3):
                fx_copy(slot, o).start()

    def turn_q(slot):
        @pl.when(rank == 2)
        def _():
            for o in (1, 3, 2):
                fx_copy(slot, o).wait_recv()
            for m in range(2):
                xt2[slot, m] = fq[slot, :, m].reshape(TOK, FEAT).T

    def send_d(n):
        @pl.when(rank < 2)
        def _():
            d_copy(n, rank, dbuf[MOVED[n]].at[blk]).start()

    def relay_d(n):
        @pl.when(rank == 1)
        def _():
            d_copy(n, 0, fd[n].at[0, blk]).wait_recv()
            d_copy(n, 0, fd[n].at[0, blk]).start()

    def collect_d(n, slot):
        @pl.when(rank == 2)
        def _():
            d_copy(n, slot, fd[n].at[slot, blk]).wait_recv()
            for o in (2, 1, 3):
                fg_copy(n, slot, o).start()
            ff_copy(n, slot, 0).start()

    def spread_d(n, slot):
        @pl.when(rank == 2)
        def _():
            for o in (1, 3, 2):
                fg_copy(n, slot, o).wait_recv()
                ff_copy(n, slot, o).start()

    def add_d(n):
        @pl.when(rank == 2)
        def _():
            lo, w = SLICES[MOVED[n]]
            for slot in range(2):
                for o in range(NY):
                    ff_copy(n, slot, o).wait_recv()
                for m in range(3):
                    term = dot(xt2[slot, m // 2], fd[n][slot, :, m].reshape(TOK, w)) * factor
                    for j in range(NZ):
                        counts = jnp.where(left, j, NZ - 1 - j) > slot
                        for v in range(w // LANE):
                            u = lo // LANE + v
                            rows = slice(m * CHUNK, (m + 1) * CHUNK)
                            more = term[j * CHUNK:(j + 1) * CHUNK, v * LANE:(v + 1) * LANE]
                            fsum[u - EARLY, j, rows, :] = (
                                fsum[u - EARLY, j, rows, :] + jnp.where(counts, more, 0.0)
                                if slot else jnp.where(counts, more, 0.0)
                            )
                            if slot:
                                zterm[u, j, rows, :] = (
                                    zterm[u, j, rows, :].astype(F32) + fsum[u - EARLY, j, rows, :]
                                ).astype(BF)

    def x_copy(o):
        return copy(xsend.at[(x + o) % NX], xrecv.at[o - 1], xs.at[o - 1], xr.at[o - 1], at_x(o))

    def hi_copy(n):
        return copy(hsend.at[n], hrecv.at[n], hs.at[n], hr.at[n], partner)

    def ag_copy(n, o):
        return copy(agbuf.at[x, n], agbuf.at[x, n], ags.at[n, o - 1], agr.at[n, o - 1], at_x(o))

    def sum_x():
        for o in (1, 3, 2):
            x_copy(o).wait_recv()
        mine = pl.ds(pl.multiple_of(x * XTOK, XTOK), XTOK)
        total = ig[mine, :]
        for o in range(3):
            total = total + xrecv[o].astype(F32)
        for n in range(PIECES):
            hsend[n] = total[n * PTOK:(n + 1) * PTOK].astype(BF)
        pl.semaphore_wait(ring, 1)

    def gather_x(n):
        hi_copy(n).wait_recv()
        agbuf[x, n] = (hsend[n].astype(F32) + hrecv[n].astype(F32)).astype(BF)
        for o in (2, 1, 3):
            ag_copy(n, o).start()

    first(0)
    send_q()
    first(1)
    reduce_core(0)
    xt[0] = x_ref[...].T
    xt[1] = g_ref[...].T
    pass_on()
    first(2)
    middle(0)
    reduce_core(1)
    pass_on()
    first(3)
    reduce_core(2)
    relay_q()
    spread(0)
    arrive(0)
    weights(0)
    z_first(0, FIRST)
    collect_q(1)
    pass_on()
    middle(1)
    reduce_core(3)
    inputs(0)
    pass_on()
    spread(1)
    arrive(1)
    weights(1)
    z_first(FIRST, SECOND)
    collect_q(0)
    pass_on()
    middle(2)
    inputs(1)
    z_steps(0, 4)
    pass_on()
    middle(3)
    send_d(0)
    spread(2)
    arrive(2)
    weights(2)
    z_first(SECOND, NEAR_STEPS)
    relay_d(0)
    inputs(2)
    pass_on()
    z_steps(4, 8)
    spread(3)
    arrive(3)
    inputs(3)
    for o in (2, 1, 3):
        x_copy(o).start()
    collect_d(0, 1)
    collect_d(0, 0)
    weights(3)
    turn_q(1)
    turn_q(0)
    z_steps(8, 14)
    sum_x()
    hi_copy(0).start()
    z_steps(14, 17)
    hi_copy(1).start()
    spread_d(0, 1)
    spread_d(0, 0)
    z_steps(17, 21)
    hi_copy(2).start()
    z_steps(21, THIRD + SKEW)
    hi_copy(3).start()
    add_d(0)
    z_steps(THIRD + SKEW, 30)
    gather_x(0)
    z_steps(30, 33)
    gather_x(1)
    z_steps(33, 36)
    gather_x(2)
    z_steps(36, 39)
    gather_x(3)
    z_steps(39, 41)

    def finish(u, carry):
        early = u < EARLY
        from_below = dep > jnp.where(early, 0, 2)
        from_above = dep < jnp.where(early, NZ - 1, NZ - 3)
        lanes = pl.ds(pl.multiple_of(u * LANE, LANE), LANE)
        wgr_ref[:, lanes] = zterm[u, dep].astype(F32)

        @pl.when(from_below)
        def _():
            z_up(u, dep).wait_recv()
            wgr_ref[:, lanes] += zl[u, dep].astype(F32)

        @pl.when(from_above)
        def _():
            z_down(u, dep).wait_recv()
            wgr_ref[:, lanes] += zr[u, dep].astype(F32)

        return carry

    lax.fori_loop(0, EARLY, finish, 0)

    for s in range(NS):
        core_copy(s).wait_send()
        for o in (1, 2, 3):
            y_copy(s, o).wait_send()
            gather_copy(s, o).wait_send()
        for o in range(NY):
            cross_copy(s, o).wait_send()
    for o in (1, 2, 3):
        x_copy(o).wait_send()
    for n in range(PIECES):
        hi_copy(n).wait_send()

    @pl.when(rank < 2)
    def _():
        q_copy(rank, ownq).wait_send()
        for n in range(NM):
            d_copy(n, rank, dbuf[MOVED[n]].at[blk]).wait_send()

    @pl.when(rank == 1)
    def _():
        q_copy(0, ownq).wait_send()
        for n in range(NM):
            d_copy(n, 0, fd[n].at[0, blk]).wait_send()

    @pl.when(rank == 2)
    def _():
        for slot in range(2):
            for o in (1, 2, 3):
                fx_copy(slot, o).wait_send()
                for n in range(NM):
                    fg_copy(n, slot, o).wait_send()
            for o in range(NY):
                for n in range(NM):
                    ff_copy(n, slot, o).wait_send()

    z_steps(41, LAST)
    for n in range(PIECES):
        for o in (1, 3, 2):
            ag_copy(n, o).wait_recv()
    out = pltpu.make_async_copy(agbuf, ig_ref, loads.at[0])
    out.start()
    lax.fori_loop(EARLY, UNITS, finish, 0)
    for n in range(PIECES):
        for o in (1, 2, 3):
            ag_copy(n, o).wait_send()

    def drain(q, carry):
        u, j = q // NZ, q % NZ
        sends = ((j > dep) & (dep >= 2)) | ((j < dep) & (dep <= NZ - 3)) | ((j != dep) & (u < EARLY))

        @pl.when(sends)
        def _():
            z_up(u, j).wait_send()

        return carry

    lax.fori_loop(0, UNITS * NZ, drain, 0)
    out.wait()


def results(ig_ref, wgr_ref, input_ref, gate_ref, up_ref, down_ref):
    input_ref[...] = ig_ref[...].astype(F32)
    gate_ref[...] = wgr_ref[:CHUNK]
    up_ref[...] = wgr_ref[CHUNK:2 * CHUNK]
    down_ref[...] = wgr_ref[2 * CHUNK:]


def shards(layer_input, output_grad, w_gate, w_up, w_down):
    factor = float(layer_input.shape[0] * lax.axis_size("depth")) ** (-0.5)
    dma = pltpu.SemaphoreType.DMA

    def per_slice(lead, dtype):
        return [pltpu.VMEM((*lead, w), dtype) for _, w in SLICES]

    scratch = [
        pltpu.VMEM((TOK, FEAT), BF),
        pltpu.VMEM((TOK, FEAT), BF),
        pltpu.VMEM((FEAT, HID), BF),
        pltpu.VMEM((FEAT, HID), BF),
        pltpu.VMEM((HID, FEAT), BF),
        dma((5,)),
        pltpu.SemaphoreType.REGULAR,
        pltpu.VMEM((2, FEAT, TOK), BF),
        *per_slice((3, HALF), F32),
        *per_slice((3, HALF), BF),
        *per_slice((3, HALF), BF),
        *per_slice((NY, 3, QUART), BF),
        *per_slice((NY - 1, 3, QUART), BF),
        *per_slice((2 * NY, 3, QUART), BF),
        pltpu.VMEM((UNITS, NZ, ROWS, LANE), BF),
        pltpu.VMEM((UNITS, NZ, ROWS, LANE), BF),
        pltpu.VMEM((UNITS, NZ, ROWS, LANE), BF),
        pltpu.VMEM((TOK, FEAT), F32),
        pltpu.VMEM((NX, XTOK, FEAT), BF),
        pltpu.VMEM((NX - 1, XTOK, FEAT), BF),
        pltpu.VMEM((PIECES, PTOK, FEAT), BF),
        pltpu.VMEM((PIECES, PTOK, FEAT), BF),
        pltpu.VMEM((NX, PIECES, PTOK, FEAT), BF),
        pltpu.VMEM((2, XTOK, FEAT), BF),
        pltpu.VMEM((2, NX, 2, XTOK, FEAT), BF),
        pltpu.VMEM((2, 2, FEAT, TOK), BF),
        pltpu.VMEM((LATE, NZ, ROWS, LANE), F32),
        *[pltpu.VMEM((2, 2 * NY, 3, QUART, SLICES[s][1]), BF) for s in MOVED],
        dma((NS,)), dma((NS,)),
        dma((NS, 3)), dma((NS, 3)),
        dma((NS, 3)), dma((NS, 3)),
        dma((NS, NY)), dma((NS, NY)),
        dma((UNITS, NZ)), dma((UNITS, NZ)), dma((UNITS, NZ)),
        dma((3,)), dma((3,)),
        dma((PIECES,)), dma((PIECES,)),
        dma((PIECES, 3)), dma((PIECES, 3)),
        dma((2,)), dma((2,)),
        dma((NM, 2)), dma((NM, 2)),
        dma((2, 3)), dma((2, 3)),
        dma((NM, 2, 3)), dma((NM, 2, 3)),
        dma((NM, 2, NY)), dma((NM, 2, NY)),
    ]
    vmem = pl.BlockSpec(memory_space=pltpu.VMEM)
    ig, wgr = pl.pallas_call(
        lambda *refs: kernel(factor, *refs),
        out_shape=(
            jax.ShapeDtypeStruct((NX, PIECES, PTOK, FEAT), BF),
            jax.ShapeDtypeStruct((ROWS, HID), F32),
        ),
        in_specs=[pl.BlockSpec(memory_space=pl.ANY)] * 5,
        out_specs=(pl.BlockSpec(memory_space=pl.ANY), vmem),
        scratch_shapes=scratch,
        compiler_params=pltpu.CompilerParams(
            collective_id=0, has_side_effects=True, vmem_limit_bytes=56 * 2 ** 20
        ),
        name="swiglu_back",
    )(layer_input, output_grad, w_gate, w_up, w_down)
    input_grad, gate_grad, up_grad, down_grad = pl.pallas_call(
        results,
        out_shape=(
            jax.ShapeDtypeStruct((TOK, FEAT), F32),
            jax.ShapeDtypeStruct((CHUNK, HID), F32),
            jax.ShapeDtypeStruct((CHUNK, HID), F32),
            jax.ShapeDtypeStruct((CHUNK, HID), F32),
        ),
        in_specs=[vmem] * 2,
        out_specs=(vmem,) * 4,
        name="results",
    )(ig.reshape(TOK, FEAT), wgr)
    return input_grad, gate_grad, up_grad, down_grad.T


def solution(mesh):
    in_specs = (
        P("depth", "row"),
        P("depth", "row"),
        P("row", "col"),
        P("row", "col"),
        P("col", "row"),
    )
    out_specs = (
        P("depth", "row"),
        P(("row", "depth"), "col"),
        P(("row", "depth"), "col"),
        P("col", ("row", "depth")),
    )
    return jax.shard_map(shards, mesh=mesh, in_specs=in_specs, out_specs=out_specs, check_vma=False)
```
